256 devices in a mesh: tm: 32 (over x, y, core), tensor: 8 (over z).
Axes of the slice: x: 4, y: 4, z: 8, core: 2. Of those that a mesh axis runs over, the one named last changes fastest.
Arguments:
- latents: float32 [32, 1024, 3072], P('tm', None, 'tensor'), may hold values from -104 to 104
- noise: bfloat16 [32, 1024, 3072], P('tm', None, 'tensor'), may hold values from -5 to 5
- qkv_weight: bfloat16 [3072, 3, 3072], P(None, None, 'tensor'), may hold values from -0.108253175 to 0.108253175
- qk_gains: float32 [2, 3072], P(None, 'tensor'), may hold values from 0.45 to 6.6
- out_weight: bfloat16 [3072, 3072], P('tensor'), may hold values from -0.109375 to 0.109375
- modulation: bfloat16 [64, 3, 3072], P(None, None, 'tensor'), may hold values from -3 to 3
- step_sizes: float32 [64], replicated, may hold values from 0.02 to 0.08
- window_start: int32 [1], replicated, may hold values from 0 to 32
Outputs:
- updated: float32 [32, 1024, 3072], P('tm', None, 'tensor')
- velocity_out: bfloat16 [32, 1024, 3072], P('tm', None, 'tensor')
- slot_errors: float32 [32], P('tm')
The draws below stay inside these ranges and needn't reach their ends.
All inputs are finite; a program needn't handle non-finite values.
Results may differ from the reference program's by a relative error of at most 0.012.
Values may be sent and summed in bfloat16 or wider, within the bound.
No kernel may reach another device: no remote copies, remote signals or barrier semaphores. Data moves between devices by JAX's collectives and lax.ppermute only.
A program may use at most 192 MiB of HBM per device.

```python
import math
import jax
import jax.numpy as jnp
from jax import lax

D = 3072
HEADS = 24
HEAD = 128
SEQ = 1024
STEPS = 64
WINDOW = 32
N_TENSOR = 8


def feature_scale(key, width):
    rising = jnp.exp(math.log(3.0) * jnp.arange(width, dtype=jnp.float32) / width)
    return rising * jax.random.uniform(key, (width,), jnp.float32, 0.6, 1.6)


def draw_latents(key, part):
    key = jax.random.fold_in(key, 11)
    key_base, key_scale = jax.random.split(key, 2)
    scale = feature_scale(key_scale, D)
    base = jax.random.truncated_normal(key_base, -4.0, 4.0, (WINDOW, SEQ, D), jnp.float32)
    return base * scale


def draw_noise(key, part):
    key = jax.random.fold_in(key, 12)
    key_base, key_scale = jax.random.split(key, 2)
    scale = 0.15 * feature_scale(key_scale, D)
    base = jax.random.truncated_normal(key_base, -4.0, 4.0, (WINDOW, SEQ, D), jnp.float32)
    return (base * scale).astype(jnp.bfloat16)


def draw_qkv_weight(key, part):
    key = jax.random.fold_in(key, 13)
    key_query, key_key, key_value = jax.random.split(key, 3)
    factor = D ** (-0.5)
    w_query = factor * jax.random.truncated_normal(key_query, -4.0, 4.0, (D, D), jnp.float32)
    w_key = factor * jax.random.truncated_normal(key_key, -4.0, 4.0, (D, D), jnp.float32)
    w_value = factor * jax.random.truncated_normal(key_value, -4.0, 4.0, (D, D), jnp.float32)
    return jnp.stack([w_query, w_key, w_value], axis=1).astype(jnp.bfloat16)


def draw_qk_gains(key, part):
    key = jax.random.fold_in(key, 14)
    key_heads, key_jitter = jax.random.split(key, 2)
    upper = math.log(2.0)
    strength = jnp.exp(jax.random.uniform(key_heads, (1, HEADS, 1), jnp.float32, math.log(0.5), upper))
    jitter = jax.random.uniform(key_jitter, (2, HEADS, HEAD), jnp.float32, 0.9, 1.1)
    return (strength * jitter).reshape(2, D)


def level_of(rng, extent, pieces, smallest, largest):
    def one(position, blocks):
        heights = jax.random.uniform(jax.random.fold_in(jax.random.fold_in(rng, 6), position), (blocks,), jnp.float32, smallest / len(pieces), largest / len(pieces))
        return jnp.repeat(jnp.exp(heights), extent[position] // blocks).reshape((-1,) + (1,) * (len(extent) - position - 1))

    level = one(*pieces[0])
    for cut in pieces[1:]:
        level = level * one(*cut)
    return level


def scatter_about(stream_key, shape, deviation, reach, cuts=(), held_as=jnp.bfloat16):
    gain = level_of(stream_key, shape, cuts, -0.22, 0.18) if cuts else 1.0
    array = jax.random.normal(stream_key, shape, jnp.float32) * deviation * gain
    return jnp.minimum(jnp.maximum(array, -reach), reach).astype(held_as)


def setup_inputs(seed: int = 0) -> dict:
    arg_keys = jax.random.split(jax.random.key(seed), 9)
    return {
        "latents": draw_latents(jax.random.fold_in(arg_keys[8], 71), 0),
        "noise": draw_noise(jax.random.fold_in(arg_keys[8], 71), 0),
        "qkv_weight": draw_qkv_weight(jax.random.fold_in(arg_keys[8], 71), 0),
        "qk_gains": draw_qk_gains(jax.random.fold_in(arg_keys[8], 71), 0),
        "out_weight": scatter_about(arg_keys[4], (D, D), D ** -0.5, 0.109375, ((0, 8),)),
        "modulation": scatter_about(arg_keys[5], (STEPS, 3, D), 0.5, 3.0, ((2, 8),)),
        "step_sizes": jnp.clip(jnp.exp(jax.random.uniform(arg_keys[6], (STEPS,), jnp.float32, math.log(0.02), math.log(0.08))), 0.02, 0.08),
        "window_start": jax.random.randint(arg_keys[7], (1,), 0, STEPS - WINDOW + 1).astype(jnp.int32),
    }


epsilon = 1e-06

def rms_scale(vectors, gain_rows):
    power = lax.optimization_barrier(jnp.mean(vectors * vectors, axis=-1, keepdims=True))
    return vectors * lax.rsqrt(power + epsilon) * gain_rows

def reference(latents, noise, qkv_weight, qk_gains, out_weight, modulation, step_sizes, window_start):
    offset = window_start[0]
    window_mod = lax.dynamic_slice_in_dim(modulation, offset, WINDOW, 0).astype(jnp.float32)
    window_steps = lax.dynamic_slice_in_dim(step_sizes, offset, WINDOW, 0)
    gain_rows = qk_gains.reshape(2, HEADS, HEAD)
    scaling = 1.0 / math.sqrt(HEAD)
    group_in = D // N_TENSOR

    def velocity_of(inputs):
        state, mod_rows = inputs
        row_mean = lax.optimization_barrier(jnp.mean(state, axis=1, keepdims=True))
        row_var = lax.optimization_barrier(jnp.mean(state * state, axis=1, keepdims=True)) - row_mean * row_mean
        modulated = ((state - row_mean) * lax.rsqrt(row_var + epsilon) * (1.0 + mod_rows[1]) + mod_rows[0]).astype(jnp.bfloat16)
        projected = jnp.dot(modulated, qkv_weight.reshape(D, 3 * D), preferred_element_type=jnp.float32)
        projected = projected.reshape(SEQ, 3, HEADS, HEAD)
        queries = rms_scale(projected[:, 0], gain_rows[0]).astype(jnp.bfloat16)
        keys_normed = rms_scale(projected[:, 1], gain_rows[1]).astype(jnp.bfloat16)
        values_heads = projected[:, 2].astype(jnp.bfloat16)
        scores = jnp.einsum('qhd,khd->hqk', queries.astype(jnp.float32), keys_normed.astype(jnp.float32)) * scaling
        attn_weights = jax.nn.softmax(scores, axis=-1).astype(jnp.bfloat16)
        attended = jnp.einsum('hqk,khd->qhd', attn_weights.astype(jnp.float32), values_heads.astype(jnp.float32))
        attended = attended.astype(jnp.bfloat16).reshape(SEQ, D)

        def group_term(group):
            start = (group * group_in).astype(jnp.int32)
            cols = lax.dynamic_slice_in_dim(attended, start, group_in, 1)
            rows = lax.dynamic_slice_in_dim(out_weight, start, group_in, 0)
            return jnp.dot(cols, rows, preferred_element_type=jnp.float32).astype(jnp.bfloat16)
        head_partials = lax.map(group_term, jnp.arange(N_TENSOR, dtype=jnp.int32))
        branch = lax.optimization_barrier(jnp.sum(head_partials.astype(jnp.float32), axis=0))
        return state + mod_rows[2] * branch
    velocity = lax.map(velocity_of, (latents, window_mod))
    increment = -window_steps[:, None, None] * velocity + noise.astype(jnp.float32)
    running = jnp.cumsum(increment, axis=0)
    earlier = jnp.concatenate([jnp.zeros((1, SEQ, D), jnp.float32), running[:-1]], axis=0)
    updated = latents[0][None] + earlier
    change = updated - latents
    slot_errors = lax.optimization_barrier(jnp.mean(change * change, axis=(1, 2)))
    return (updated, velocity.astype(jnp.bfloat16), slot_errors)
```

```python
import functools
import math

import jax
import jax.numpy as jnp
from jax import lax
from jax.experimental import pallas as pl
from jax.experimental.pallas import tpu as pltpu
from jax.sharding import PartitionSpec as P

HEAD = 128
LEVELS = 8
SIDE = 4
AUX = 16
epsilon = 1e-06
F32 = jnp.float32
BF16 = jnp.bfloat16
MIB = 1 << 20


def shift_z(value, step):
    return lax.ppermute(value, "tensor", [(i, (i + step) % LEVELS) for i in range(LEVELS)])


def tm_place(x, y, core):
    return (x % SIDE * SIDE + y % SIDE) * 2 + core


def shift_tm(value, dx, dy, swap):
    pairs = [
        (tm_place(x, y, c), tm_place(x + dx, y + dy, c ^ swap))
        for x in range(SIDE)
        for y in range(SIDE)
        for c in range(2)
    ]
    return lax.ppermute(value, "tm", pairs)


def params(mib):
    return pltpu.CompilerParams(vmem_limit_bytes=mib * MIB)


def cost(flops, moved):
    return pl.CostEstimate(flops=int(flops), bytes_accessed=int(moved), transcendentals=0)


def ring_gather(top, bottom):
    up_top, up_bottom, down_top, down_bottom = top, bottom, top, bottom
    arrivals = []
    for step in range(1, LEVELS // 2):
        up_top, down_bottom = shift_z(up_top, 1), shift_z(down_bottom, -1)
        up_bottom, down_top = shift_z(up_bottom, 1), shift_z(down_top, -1)
        arrivals.append([(up_top, up_bottom), (down_top, down_bottom)])
    arrivals.append([(shift_z(up_top, 1), shift_z(down_bottom, -1))])
    return arrivals


def scale_chunk(top, bottom, scaled, column, s1_ref, s2_ref, fresh):
    half = bottom.shape[0]
    width = bottom.shape[1]
    lanes = pl.ds(column * width, width)
    aux = top[half : half + AUX, :].astype(F32)
    gain = 1.0 + aux[0:1]
    for part in range(2):
        piece = (top, bottom)[part]
        for block in range(half // 128):
            rows = pl.ds(part * half + block * 128, 128)
            x = piece[block * 128 : (block + 1) * 128, :].astype(F32)
            scaled[rows, lanes] = (x * gain).astype(BF16)
            square = x * x
            total, squares = x[:, :HEAD], square[:, :HEAD]
            for lane in range(HEAD, width, HEAD):
                total = total + x[:, lane : lane + HEAD]
                squares = squares + square[:, lane : lane + HEAD]
            if fresh:
                s1_ref[rows, :] = total
                s2_ref[rows, :] = squares
            else:
                s1_ref[rows, :] += total
                s2_ref[rows, :] += squares
    row = lax.broadcasted_iota(jnp.int32, (AUX, width), 0)
    high = gain.astype(BF16).astype(F32)
    extra = jnp.where(row == 0, high, jnp.where(row == 1, gain - high, jnp.where(row == 2, aux[1:2], 0.0)))
    scaled[pl.ds(2 * half, AUX), lanes] = extra.astype(BF16)


def project_kernel(count, has_state, *refs):
    refs = list(refs[1:])
    chunks = [(refs[2 * i], refs[2 * i + 1]) for i in range(count)]
    weights = refs[2 * count : 3 * count]
    refs = refs[3 * count :]
    if has_state:
        acc_in, s1_in, s2_in = refs[:3]
        refs = refs[3:]
    acc, s1, s2, scaled = refs
    width = weights[0].shape[1]

    @pl.when(pl.program_id(0) == 0)
    def _():
        if has_state:
            s1[...] = s1_in[...]
            s2[...] = s2_in[...]
        for i, (top, bottom) in enumerate(chunks):
            scale_chunk(top, bottom, scaled, i, s1, s2, not has_state and i == 0)

    tile = acc.shape[1] // 5

    @pl.loop(0, 5)
    def _(step):
        rows = pl.ds(pl.multiple_of(step * tile, AUX), tile)
        total = acc_in[0, rows, :] if has_state else None
        for i in range(count):
            part = jnp.dot(
                scaled[rows, i * width : (i + 1) * width], weights[i][0], preferred_element_type=F32
            )
            total = part if total is None else total + part
        acc[0, rows, :] = total


def project(chunks, sources, weight, state):
    count = len(chunks)
    half, width = chunks[0][1].shape
    rows = 2 * half + AUX
    whole = lambda j, s: (0, 0)
    in_specs = [
        pl.BlockSpec((half + AUX, width), whole) if part == 0 else pl.BlockSpec((half, width), whole)
        for _ in range(count)
        for part in range(2)
    ]
    in_specs += [pl.BlockSpec((1, width, width), lambda j, s, i=i: (j, s[i], 0)) for i in range(count)]
    acc_spec = pl.BlockSpec((1, rows, width), lambda j, s: (j, 0, 0))
    sum_spec = pl.BlockSpec((2 * half, HEAD), whole)
    operands = [piece for chunk in chunks for piece in chunk] + [weight] * count
    aliases = {}
    if state is not None:
        first = 1 + len(operands)
        aliases = {first: 0, first + 1: 1, first + 2: 2}
        in_specs += [acc_spec, sum_spec, sum_spec]
        operands += list(state)
    return pl.pallas_call(
        functools.partial(project_kernel, count, state is not None),
        grid_spec=pltpu.PrefetchScalarGridSpec(
            num_scalar_prefetch=1,
            grid=(3,),
            in_specs=in_specs,
            out_specs=[acc_spec, sum_spec, sum_spec],
            scratch_shapes=[pltpu.VMEM((rows, count * width), BF16)],
        ),
        out_shape=[
            jax.ShapeDtypeStruct((3, rows, width), F32),
            jax.ShapeDtypeStruct((2 * half, HEAD), F32),
            jax.ShapeDtypeStruct((2 * half, HEAD), F32),
        ],
        input_output_aliases=aliases,
        compiler_params=params(32),
        cost_estimate=cost(2 * rows * width * 3 * width * count, 12 * MIB),
        name="project",
    )(sources, *operands)


def finish_kernel(features, src, top, bottom, weight, acc_in, s1_in, s2_in, gains, out, scaled, s1, s2, mean, rstd):
    slot = pl.program_id(0)
    length, width = out.shape[1], out.shape[2]

    @pl.when(slot == 0)
    def _():
        s1[...] = s1_in[...]
        s2[...] = s2_in[...]
        scale_chunk(top, bottom, scaled, 0, s1, s2, False)
        average = jnp.sum(s1[...], axis=1, keepdims=True) * (1.0 / features)
        power = jnp.sum(s2[...], axis=1, keepdims=True) * (1.0 / features)
        mean[...] = average
        rstd[...] = lax.rsqrt(power - average * average + epsilon)

    extra = acc_in[0, length:, :] + jnp.dot(scaled[length:, :], weight[0], preferred_element_type=F32)
    gain_product = extra[0:1] + extra[1:2]
    shift_product = extra[2:3]
    is_value = slot == 2
    gain_row = gains[0]
    tile = 256

    @pl.loop(0, length // tile)
    def _(step):
        rows = pl.ds(pl.multiple_of(step * tile, tile), tile)
        total = acc_in[0, rows, :] + jnp.dot(scaled[rows, :], weight[0], preferred_element_type=F32)
        total = rstd[rows, :] * (total - mean[rows, :] * gain_product) + shift_product
        for lane in range(0, width, HEAD):
            vectors = total[:, lane : lane + HEAD]
            power = jnp.mean(vectors * vectors, axis=1, keepdims=True)
            normed = vectors * lax.rsqrt(power + epsilon) * gain_row[:, lane : lane + HEAD]
            out[0, rows, lane : lane + HEAD] = jnp.where(is_value, vectors, normed).astype(BF16)


def finish(chunk, source, weight, state, gains, features):
    top, bottom = chunk
    half, width = bottom.shape
    rows = 2 * half + AUX
    whole = lambda j, s: (0, 0)
    return pl.pallas_call(
        functools.partial(finish_kernel, features),
        grid_spec=pltpu.PrefetchScalarGridSpec(
            num_scalar_prefetch=1,
            grid=(3,),
            in_specs=[
                pl.BlockSpec((half + AUX, width), whole),
                pl.BlockSpec((half, width), whole),
                pl.BlockSpec((1, width, width), lambda j, s: (j, s[0], 0)),
                pl.BlockSpec((1, rows, width), lambda j, s: (j, 0, 0)),
                pl.BlockSpec((2 * half, HEAD), whole),
                pl.BlockSpec((2 * half, HEAD), whole),
                pl.BlockSpec((1, 1, width), lambda j, s: (j, 0, 0)),
            ],
            out_specs=pl.BlockSpec((1, 2 * half, width), lambda j, s: (j, 0, 0)),
            scratch_shapes=[
                pltpu.VMEM((rows, width), BF16),
                pltpu.VMEM((2 * half, HEAD), F32),
                pltpu.VMEM((2 * half, HEAD), F32),
                pltpu.VMEM((2 * half, 1), F32),
                pltpu.VMEM((2 * half, 1), F32),
            ],
        ),
        out_shape=jax.ShapeDtypeStruct((3, 2 * half, width), BF16),
        compiler_params=params(32),
        cost_estimate=cost(2 * rows * width * 3 * width, 8 * MIB),
        name="finish",
    )(source, top, bottom, weight, *state, gains)


def attend_kernel(count, dest, *refs):
    queries = refs[:count]
    keys, values = refs[count][0], refs[count + 1][0]
    outs = refs[count + 2 :]
    for first in range(0, count, 2):
        group = range(first, min(first + 2, count))
        rows = jnp.concatenate([queries[i][0] for i in group], axis=0)
        scores = lax.dot_general(rows, keys, (((1,), (1,)), ((), ())), preferred_element_type=F32)
        weights = jnp.exp2(scores - jnp.max(scores, axis=1, keepdims=True))
        total = jnp.sum(weights, axis=1, keepdims=True)
        mixed = jnp.dot(weights.astype(BF16), values, preferred_element_type=F32) / total
        for place, i in enumerate(group):
            outs[i][...] = mixed[place * 128 : (place + 1) * 128].astype(BF16)


def attend(qkv, dest):
    count = dest.shape[0]
    _, length, width = qkv.shape
    block = length // LEVELS
    in_specs = [pl.BlockSpec((1, block, HEAD), lambda h, d, i=i: (0, d[i], h)) for i in range(count)]
    in_specs += [pl.BlockSpec((1, length, HEAD), lambda h, d, j=j: (j, 0, h)) for j in (1, 2)]
    return pl.pallas_call(
        functools.partial(attend_kernel, count),
        grid_spec=pltpu.PrefetchScalarGridSpec(
            num_scalar_prefetch=1,
            grid=(width // HEAD,),
            in_specs=in_specs,
            out_specs=[pl.BlockSpec((block, HEAD), lambda h, d: (0, h)) for _ in range(count)],
        ),
        out_shape=[jax.ShapeDtypeStruct((block, width), BF16) for _ in range(count)],
        compiler_params=params(32),
        cost_estimate=cost(8 * count * block * length * width, 3 * MIB),
        name="attend",
    )(dest, *([qkv] * (count + 2)))


def mix_kernel(count, dest, *refs):
    inputs, weight, outs = refs[:LEVELS], refs[LEVELS], refs[LEVELS + 1 :]
    total = None
    for k in range(LEVELS):
        rows = jnp.concatenate([weight[a, k] for a in range(4)], axis=0)
        part = jnp.dot(inputs[k][...], rows, preferred_element_type=F32)
        total = part if total is None else total + part
    total = total.astype(BF16)
    for i in range(count):

        @pl.when(pl.program_id(0) == i)
        def _(i=i):
            outs[i][...] = total


def mix(inputs, weight, dest):
    count = dest.shape[0]
    block, width = inputs[0].shape
    whole = lambda i, d: (0, 0)
    return pl.pallas_call(
        functools.partial(mix_kernel, count),
        grid_spec=pltpu.PrefetchScalarGridSpec(
            num_scalar_prefetch=1,
            grid=(count,),
            in_specs=[pl.BlockSpec((block, width), whole) for _ in range(LEVELS)]
            + [pl.BlockSpec((4, LEVELS, width // 4, width), lambda i, d: (d[i], 0, 0, 0))],
            out_specs=[pl.BlockSpec((block, width), whole) for _ in range(count)],
        ),
        out_shape=[jax.ShapeDtypeStruct((block, width), BF16) for _ in range(count)],
        compiler_params=params(32),
        cost_estimate=cost(2 * count * block * width * width * LEVELS, 3 * MIB * count),
        name="mix",
    )(dest, *inputs, weight)


def update_kernel(dest, scalars, *refs):
    branches, (latents, noise, gate, velocity_out, increment_out) = refs[:LEVELS], refs[LEVELS:]
    step_size, first = scalars[0], scalars[1]
    for k in range(LEVELS):

        @pl.when(pl.program_id(0) == k)
        def _(k=k):
            x = latents[0]
            velocity = x + gate[...] * branches[k][...].astype(F32)
            velocity_out[0] = velocity.astype(BF16)
            increment = first * x - step_size * velocity + noise[0].astype(F32)
            increment_out[...] = increment.astype(BF16)


def update(branches, places, scalars, latents, noise, gate):
    block, width = branches[0].shape
    length = latents.shape[1]
    whole = lambda i, d, s: (0, 0)
    placed = lambda i, d, s: (0, d[i], 0)
    return pl.pallas_call(
        update_kernel,
        grid_spec=pltpu.PrefetchScalarGridSpec(
            num_scalar_prefetch=2,
            grid=(LEVELS,),
            in_specs=[pl.BlockSpec((block, width), whole) for _ in range(LEVELS)]
            + [
                pl.BlockSpec((1, block, width), placed),
                pl.BlockSpec((1, block, width), placed),
                pl.BlockSpec((1, width), whole),
            ],
            out_specs=[
                pl.BlockSpec((1, block, width), placed),
                pl.BlockSpec((block, width), lambda i, d, s: (d[i], 0)),
            ],
        ),
        out_shape=[
            jax.ShapeDtypeStruct((1, length, width), BF16),
            jax.ShapeDtypeStruct((length, width), BF16),
        ],
        compiler_params=params(16),
        cost_estimate=cost(8 * length * width, 5 * MIB),
        name="update",
    )(places, scalars, *branches, latents, noise, gate)


def exclusive_prefix(increment, slot):
    core, y, x = slot % 2, slot // 2 % SIDE, slot // (2 * SIDE)
    length, width = increment.shape
    half = length // 2
    halves = increment.reshape(2, half, width)
    kept = lax.dynamic_index_in_dim(halves, core, 0, False)
    other = shift_tm(lax.dynamic_index_in_dim(halves, 1 - core, 0, False), 0, 0, 1)
    chip_sum = (kept.astype(F32) + other.astype(F32)).astype(BF16)
    earlier = jnp.where(core == 0, kept, other).astype(F32)
    pieces = chip_sum.reshape(SIDE, half // SIDE, width)
    pick = lambda k: lax.dynamic_index_in_dim(pieces, (y + k) % SIDE, 0, False)
    sums = [pick(0)] + [shift_tm(pick(k), 0, k, 0) for k in range(1, SIDE)]
    sums = [piece.astype(F32) for piece in sums]
    row_sum = sum(sums[1:], sums[0]).astype(BF16)
    before = 0.0
    for k in range(1, SIDE):
        before = before + jnp.where(x >= k, shift_tm(row_sum, k, 0, 0), 0.0).astype(F32)
    prefixes = []
    for k in range(SIDE):
        total = before
        for source in range(SIDE):
            total = total + jnp.where((y - source) % SIDE < (y + k) % SIDE, sums[source], 0.0)
        prefixes.append(total.astype(BF16))
    mine = [prefixes[0]] + [shift_tm(prefixes[k], 0, k, 0) for k in range(1, SIDE)]
    placed = []
    for place in range(SIDE):
        back = (y - place) % SIDE
        piece = mine[0]
        for k in range(1, SIDE):
            piece = jnp.where(back == k, mine[k], piece)
        placed.append(piece)
    prefix = jnp.concatenate(placed, axis=0).astype(F32)
    later = prefix + earlier
    sent = jnp.where(core == 0, later, prefix).astype(BF16)
    own = jnp.where(core == 0, prefix, later)
    received = shift_tm(sent, 0, 0, 1).astype(F32)
    return jnp.concatenate([jnp.where(core == 0, own, received), jnp.where(core == 0, received, own)], axis=0)


def body(latents, noise, qkv_weight, qk_gains, out_weight, modulation, step_sizes, window_start):
    slot = lax.axis_index("tm")
    level = lax.axis_index("tensor")
    offset = window_start[0] + slot
    mod_row = lax.dynamic_index_in_dim(jnp.transpose(modulation, (1, 0, 2)), offset, 1, keepdims=False)
    step_size = lax.dynamic_index_in_dim(step_sizes, offset, 0, keepdims=False)
    own_rows = latents[0]
    length, width = own_rows.shape
    features = width * LEVELS
    half = length // 2
    at = lambda *offsets: jnp.stack([(level + k) % LEVELS for k in offsets]).astype(jnp.int32)

    share = lax.dynamic_slice(
        out_weight, (slot % 4 * (width // 4), slot // 4 * width), (width // 4, width)
    )
    up, down, rows_up, rows_down = share, share, [], []
    for step in range(1, LEVELS // 2):
        up, down = shift_z(up, 1), shift_z(down, -1)
        rows_up.append(up)
        rows_down.append(down)
    ring_rows = [share] + rows_up + [shift_z(up, 1)] + rows_down[::-1]
    whole_weight = lax.all_gather(jnp.stack(ring_rows), "tm", axis=0)

    aux = jnp.concatenate([mod_row[1:2], mod_row[0:1], jnp.zeros((AUX - 2, width), BF16)], axis=0)
    rounded = own_rows.astype(BF16)
    top, bottom = jnp.concatenate([rounded[:half], aux], axis=0), rounded[half:]
    weight = jnp.transpose(qkv_weight, (1, 0, 2))
    arrivals = ring_gather(top, bottom)
    state = project([(top, bottom)], at(0), weight, None)
    for step in range(1, LEVELS // 2):
        state = project(arrivals[step - 1], at(-step, step), weight, state)
    query_scale = math.log2(math.e) / math.sqrt(HEAD)
    gains = jnp.stack([qk_gains[0] * query_scale, qk_gains[1], jnp.ones_like(qk_gains[0])])[:, None]
    qkv = finish(arrivals[-1][0], at(LEVELS // 2), weight, state, gains, features)

    orders = ((4, 3, 5), (2, 6, 1, 7, 0))
    received = [None] * LEVELS
    for order in orders:
        for k, value in zip(order, attend(qkv, at(*order))):
            received[k] = shift_z(value, k) if k else value
    branches = [None] * LEVELS
    for order in orders:
        for k, value in zip(order, mix(received, whole_weight.reshape(32, LEVELS, width // 4, width), at(*order))):
            branches[k] = shift_z(value, k) if k else value
    is_first = slot == 0
    scalars = jnp.stack([step_size, is_first.astype(F32)])
    velocity, increment = update(
        branches, at(*[-k for k in range(LEVELS)]), scalars, latents, noise, mod_row[2:3].astype(F32)
    )
    prefix = exclusive_prefix(increment, slot)
    updated = jnp.where(is_first, own_rows, prefix)
    change = updated - own_rows
    slot_err = lax.psum(jnp.sum(change * change), "tensor") / (length * features)
    return updated[None], velocity, slot_err.reshape(1)


def solution(mesh):
    return jax.shard_map(
        body,
        mesh=mesh,
        in_specs=(
            P("tm", None, "tensor"),
            P("tm", None, "tensor"),
            P(None, None, "tensor"),
            P(None, "tensor"),
            P("tensor", None),
            P(None, None, "tensor"),
            P(),
            P(),
        ),
        out_specs=(P("tm", None, "tensor"), P("tm", None, "tensor"), P("tm")),
        check_vma=False,
    )
```

```python
import functools
import math

import jax
import jax.numpy as jnp
from jax import lax
from jax.experimental import pallas as pl
from jax.experimental.pallas import tpu as pltpu
from jax.sharding import PartitionSpec as P

HEAD = 128
LEVELS = 8
SIDE = 4
AUX = 16
epsilon = 1e-06
F32 = jnp.float32
BF16 = jnp.bfloat16
MIB = 1 << 20


def shift_z(value, step):
    return lax.ppermute(value, "tensor", [(i, (i + step) % LEVELS) for i in range(LEVELS)])


def tm_place(x, y, core):
    return (x % SIDE * SIDE + y % SIDE) * 2 + core


def shift_tm(value, dx, dy, swap):
    pairs = [
        (tm_place(x, y, c), tm_place(x + dx, y + dy, c ^ swap))
        for x in range(SIDE)
        for y in range(SIDE)
        for c in range(2)
    ]
    return lax.ppermute(value, "tm", pairs)


def params(mib):
    return pltpu.CompilerParams(vmem_limit_bytes=mib * MIB)


def cost(flops, moved):
    return pl.CostEstimate(flops=int(flops), bytes_accessed=int(moved), transcendentals=0)


def scale_chunk(top, bottom, scaled, column, s1_ref, s2_ref, fresh):
    half = bottom.shape[0]
    width = bottom.shape[1]
    lanes = pl.ds(column * width, width)
    aux = top[half : half + AUX, :].astype(F32)
    gain = 1.0 + aux[0:1]
    for part in range(2):
        piece = (top, bottom)[part]
        for block in range(half // 128):
            rows = pl.ds(part * half + block * 128, 128)
            x = piece[block * 128 : (block + 1) * 128, :].astype(F32)
            scaled[rows, lanes] = (x * gain).astype(BF16)
            square = x * x
            total, squares = x[:, :HEAD], square[:, :HEAD]
            for lane in range(HEAD, width, HEAD):
                total = total + x[:, lane : lane + HEAD]
                squares = squares + square[:, lane : lane + HEAD]
            if fresh:
                s1_ref[rows, :] = total
                s2_ref[rows, :] = squares
            else:
                s1_ref[rows, :] += total
                s2_ref[rows, :] += squares
    row = lax.broadcasted_iota(jnp.int32, (AUX, width), 0)
    high = gain.astype(BF16).astype(F32)
    extra = jnp.where(row == 0, high, jnp.where(row == 1, gain - high, jnp.where(row == 2, aux[1:2], 0.0)))
    scaled[pl.ds(2 * half, AUX), lanes] = extra.astype(BF16)


def project_kernel(count, has_state, sources, weight, *refs):
    refs = list(refs)
    chunks = [(refs[2 * i], refs[2 * i + 1]) for i in range(count)]
    refs = refs[2 * count :]
    if has_state:
        acc_in, s1_in, s2_in = refs[:3]
        refs = refs[3:]
    acc, s1, s2, scaled = refs
    width = weight.shape[2]
    if has_state:
        s1[...] = s1_in[...]
        s2[...] = s2_in[...]
    for i, (top, bottom) in enumerate(chunks):
        scale_chunk(top, bottom, scaled, i, s1, s2, not has_state and i == 0)
    starts = [pl.multiple_of(sources[i] * width, width) for i in range(count)]
    for j in range(3):
        rows = jnp.concatenate([weight[j, pl.ds(start, width), :] for start in starts], axis=0)
        total = jnp.dot(scaled[...], rows, preferred_element_type=F32)
        acc[j] = acc_in[j] + total if has_state else total


def whole_vmem(count):
    return [pl.BlockSpec(memory_space=pltpu.VMEM)] * count


SMEM = pl.BlockSpec(memory_space=pltpu.SMEM)
HBM = pl.BlockSpec(memory_space=pltpu.HBM)


def project(chunks, sources, weight, state):
    count = len(chunks)
    half, width = chunks[0][1].shape
    rows = 2 * half + AUX
    operands = [weight] + [piece for chunk in chunks for piece in chunk]
    aliases = {}
    if state is not None:
        first = 1 + len(operands)
        aliases = {first: 0, first + 1: 1, first + 2: 2}
        operands += list(state)
    return pl.pallas_call(
        functools.partial(project_kernel, count, state is not None),
        in_specs=[pl.BlockSpec(memory_space=pltpu.SMEM)] + whole_vmem(len(operands)),
        out_specs=whole_vmem(3),
        scratch_shapes=[pltpu.VMEM((rows, count * width), BF16)],
        out_shape=[
            jax.ShapeDtypeStruct((3, rows, width), F32),
            jax.ShapeDtypeStruct((2 * half, HEAD), F32),
            jax.ShapeDtypeStruct((2 * half, HEAD), F32),
        ],
        input_output_aliases=aliases,
        compiler_params=params(16),
        cost_estimate=cost(2e9 * count, 4 * MIB),
        name="project",
    )(sources, *operands)


def finish_kernel(features, sources, weight, top, bottom, acc_in, s1, s2, gains, out, scaled, sums):
    length, width = out.shape[1], out.shape[2]
    sums[0] = s1[...]
    sums[1] = s2[...]
    scale_chunk(top, bottom, scaled, 0, sums.at[0], sums.at[1], False)
    mean = jnp.sum(sums[0], axis=1, keepdims=True) * (1.0 / features)
    power = jnp.sum(sums[1], axis=1, keepdims=True) * (1.0 / features)
    rstd = lax.rsqrt(power - mean * mean + epsilon)
    source = pl.ds(pl.multiple_of(sources[0] * width, width), width)
    for j in range(3):
        total = acc_in[j] + jnp.dot(scaled[...], weight[j, source, :], preferred_element_type=F32)
        extra = total[length:, :]
        gain_product = extra[0:1] + extra[1:2]
        total = rstd * (total[:length, :] - mean * gain_product) + extra[2:3]
        for lane in range(0, width, HEAD):
            vectors = total[:, lane : lane + HEAD]
            if j < 2:
                square = jnp.mean(vectors * vectors, axis=1, keepdims=True)
                vectors = vectors * lax.rsqrt(square + epsilon) * gains[j : j + 1, lane : lane + HEAD]
            out[j, :, lane : lane + HEAD] = vectors.astype(BF16)


def finish(chunk, source, weight, state, gains, features):
    top, bottom = chunk
    half, width = bottom.shape
    rows = 2 * half + AUX
    return pl.pallas_call(
        functools.partial(finish_kernel, features),
        in_specs=[pl.BlockSpec(memory_space=pltpu.SMEM)] + whole_vmem(7),
        out_specs=pl.BlockSpec(memory_space=pltpu.VMEM),
        scratch_shapes=[pltpu.VMEM((rows, width), BF16), pltpu.VMEM((2, 2 * half, HEAD), F32)],
        out_shape=jax.ShapeDtypeStruct((3, 2 * half, width), BF16),
        compiler_params=params(16),
        cost_estimate=cost(4e9, 4 * MIB),
        name="finish",
    )(source, weight, top, bottom, *state, gains)


def attend_kernel(place, qkv, out):
    tile = 256
    rows, width = out.shape
    for lane in range(0, width, HEAD):
        lanes = slice(lane, lane + HEAD)
        keys, values = qkv[1, :, lanes], qkv[2, :, lanes]
        for first in range(0, rows, tile):
            queries = qkv[0, pl.ds(pl.multiple_of(place[0] * rows + first, tile), tile), lanes]
            scores = lax.dot_general(queries, keys, (((1,), (1,)), ((), ())), preferred_element_type=F32)
            weights = jnp.exp2(scores - jnp.max(scores, axis=1, keepdims=True))
            total = jnp.sum(weights, axis=1, keepdims=True)
            mixed = jnp.dot(weights.astype(BF16), values, preferred_element_type=F32) / total
            out[first : first + tile, lanes] = mixed.astype(BF16)


def attend(qkv, place):
    _, length, width = qkv.shape
    return pl.pallas_call(
        attend_kernel,
        in_specs=[pl.BlockSpec(memory_space=pltpu.SMEM)] + whole_vmem(1),
        out_specs=pl.BlockSpec(memory_space=pltpu.VMEM),
        out_shape=jax.ShapeDtypeStruct((length // 2, width), BF16),
        compiler_params=params(16),
        cost_estimate=cost(4e9, 3 * MIB),
        name="attend",
    )(place, qkv)


def partial_kernel(has_sum, dest, attended, weight, *refs):
    count = len(has_sum)
    width = attended.shape[1]
    sums, outs = refs[:-count], refs[-count:]
    place = 0
    for i in range(count):
        columns = pl.ds(pl.multiple_of(dest[i] * width, width), width)
        total = jnp.dot(attended[...], weight[:, columns], preferred_element_type=F32)
        if has_sum[i]:
            total = total + sums[place][...].astype(F32)
            place += 1
        outs[i][...] = total.astype(BF16)


def partial(attended, weight, dest, sums):
    rows, width = attended.shape
    has_sum = [value is not None for value in sums]
    given = [value for value in sums if value is not None]
    return pl.pallas_call(
        functools.partial(partial_kernel, has_sum),
        in_specs=[pl.BlockSpec(memory_space=pltpu.SMEM)] + whole_vmem(2 + len(given)),
        out_specs=whole_vmem(len(sums)),
        out_shape=[jax.ShapeDtypeStruct((rows, width), BF16)] * len(sums),
        compiler_params=params(16),
        cost_estimate=cost(1e9, 2 * MIB),
        name="partial",
    )(dest, attended, weight, *given)


def update_kernel(places, scalars, own, from_below, from_above, gate, latents, noise, *refs):
    velocity_out, increment_out, x, noise_rows, arrived = refs[-5:]
    rows = own.shape[0]
    held = pl.ds(pl.multiple_of(places[0] * rows, rows), rows)
    copies = [
        pltpu.make_async_copy(latents.at[0, held, :], x, arrived.at[0]),
        pltpu.make_async_copy(noise.at[0, held, :], noise_rows, arrived.at[1]),
    ]
    for copy in copies:
        copy.start()
    branch = own[...].astype(F32) + from_below[...].astype(F32) + from_above[...].astype(F32)
    branch = gate[...] * branch
    for copy in copies:
        copy.wait()
    velocity = x[...] + branch
    velocity_out[0] = velocity.astype(BF16)
    increment = scalars[1] * x[...] - scalars[0] * velocity + noise_rows[...].astype(F32)
    increment_out[...] = increment.astype(BF16)


def update(place, scalars, own, sums, gate, latents, noise, velocity):
    rows, width = own.shape
    operands = [own, *sums, gate, latents, noise]
    in_specs = [SMEM] + whole_vmem(4) + [HBM, HBM]
    aliases = {}
    if velocity is not None:
        aliases = {2 + len(operands): 0}
        operands.append(velocity)
        in_specs.append(pl.BlockSpec(memory_space=pl.ANY))
    return pl.pallas_call(
        update_kernel,
        grid_spec=pltpu.PrefetchScalarGridSpec(
            num_scalar_prefetch=1,
            grid=(1,),
            in_specs=in_specs,
            out_specs=[pl.BlockSpec((1, rows, width), lambda i, p: (0, p[0], 0))] + whole_vmem(1),
            scratch_shapes=[
                pltpu.VMEM((rows, width), F32),
                pltpu.VMEM((rows, width), BF16),
                pltpu.SemaphoreType.DMA((2,)),
            ],
        ),
        out_shape=[
            jax.ShapeDtypeStruct((1, 2 * rows, width), BF16),
            jax.ShapeDtypeStruct((rows, width), BF16),
        ],
        input_output_aliases=aliases,
        compiler_params=params(16),
        cost_estimate=cost(1e9, 3 * MIB),
        name="update",
    )(place, scalars, *operands)


def vmem_call(kernel, name, out_shape, scalars, *operands):
    return pl.pallas_call(
        kernel,
        in_specs=[pl.BlockSpec(memory_space=pltpu.SMEM)] + whole_vmem(len(operands)),
        out_specs=whole_vmem(len(out_shape)),
        out_shape=out_shape,
        compiler_params=params(8),
        cost_estimate=cost(1e9, MIB),
        name=name,
    )(scalars, *operands)


def chip_sum_kernel(where, kept, other, *pieces):
    rows = pieces[0].shape[0]
    for k in range(SIDE):
        part = pl.ds(pl.multiple_of((where[1] + k) % SIDE * rows, rows), rows)
        pieces[k][...] = (kept[part, :].astype(F32) + other[part, :].astype(F32)).astype(BF16)


def row_sum_kernel(where, *refs):
    total = refs[0][...].astype(F32)
    for ref in refs[1:-1]:
        total = total + ref[...].astype(F32)
    refs[-1][...] = total.astype(BF16)


def prefix_kernel(where, *refs):
    x, y = where[0], where[1]
    sums = [ref[...].astype(F32) for ref in refs[:SIDE]]
    before = jnp.zeros_like(sums[0])
    for k in range(1, SIDE):
        before = before + jnp.where(x >= k, refs[SIDE + k - 1][...].astype(F32), 0.0)
    outs = refs[2 * SIDE - 1 :]
    for k in range(SIDE):
        total = before
        for source in range(SIDE):
            total = total + jnp.where((y + SIDE - source) % SIDE < (y + k) % SIDE, sums[source], 0.0)
        outs[k][...] = total.astype(BF16)


def change_kernel(places, where, *refs):
    mine, (kept, other, latents, given_rows) = refs[:SIDE], refs[SIDE : SIDE + 4]
    updated, sent, squares, kept_rows, other_rows, arrived = refs[SIDE + 4 :]
    rows, width = mine[0].shape
    held = pl.ds(pl.multiple_of(places[0] * SIDE * rows, SIDE * rows), SIDE * rows)
    copies = [
        pltpu.make_async_copy(latents.at[0, held, :], kept_rows, arrived.at[0]),
        pltpu.make_async_copy(given_rows, other_rows, arrived.at[1]),
    ]
    for copy in copies:
        copy.start()
    for copy in copies:
        copy.wait()
    y, core, chip = where[1], where[2], where[3]
    first_core, first_chip = core == 0, chip == 0
    totals = [jnp.zeros((8, HEAD), F32), jnp.zeros((8, HEAD), F32)]
    for k in range(SIDE):
        part = pl.ds(pl.multiple_of((y + SIDE - k) % SIDE * rows, rows), rows)
        even = mine[k][...].astype(F32)
        own_increment, other_increment = kept[part, :].astype(F32), other[part, :].astype(F32)
        own_x, other_x = kept_rows[part, :], other_rows[part, :]
        odd = even + jnp.where(first_core, own_increment, other_increment)
        even = jnp.where(first_chip, jnp.where(first_core, own_x, other_x), even)
        sent[part, :] = jnp.where(first_core, odd, even).astype(BF16)
        updated[0, part, :] = jnp.where(first_core, even, odd)
        changes = (
            even - jnp.where(first_core, own_x, other_x),
            odd - jnp.where(first_core, other_x, own_x),
        )
        for i, change in enumerate(changes):
            square = (change * change).reshape(rows // 8, 8, width)
            square = jnp.sum(square, axis=0)
            for lane in range(0, width, HEAD):
                totals[i] = totals[i] + square[:, lane : lane + HEAD]
    squares[0:8, :] = totals[0]
    squares[8:16, :] = totals[1]


def change(place, where, mine, kept, other, latents, other_rows):
    half, width = kept.shape
    operands = [*mine, kept, other, latents, other_rows]
    return pl.pallas_call(
        change_kernel,
        grid_spec=pltpu.PrefetchScalarGridSpec(
            num_scalar_prefetch=1,
            grid=(1,),
            in_specs=[SMEM] + whole_vmem(SIDE + 2) + [HBM, HBM],
            out_specs=[pl.BlockSpec((1, half, width), lambda i, p: (0, p[0], 0))] + whole_vmem(2),
            scratch_shapes=[
                pltpu.VMEM((half, width), F32),
                pltpu.VMEM((half, width), F32),
                pltpu.SemaphoreType.DMA((2,)),
            ],
        ),
        out_shape=[
            jax.ShapeDtypeStruct((1, 2 * half, width), F32),
            jax.ShapeDtypeStruct((half, width), BF16),
            jax.ShapeDtypeStruct((16, HEAD), F32),
        ],
        compiler_params=params(16),
        cost_estimate=cost(1e9, 3 * MIB),
        name="change",
    )(place, where, *operands)


def place_kernel(places, where, received, x, _, updated):
    first = jnp.logical_and(where[2] == 0, where[3] == 0)
    updated[0] = jnp.where(first, x[0], received[...].astype(F32))


def put_half(place, where, received, latents, updated):
    half, width = received.shape
    block = pl.BlockSpec((1, half, width), lambda i, p: (0, p[0], 0))
    return pl.pallas_call(
        place_kernel,
        grid_spec=pltpu.PrefetchScalarGridSpec(
            num_scalar_prefetch=1,
            grid=(1,),
            in_specs=[SMEM, pl.BlockSpec(memory_space=pltpu.VMEM), block, pl.BlockSpec(memory_space=pl.ANY)],
            out_specs=block,
        ),
        out_shape=jax.ShapeDtypeStruct(updated.shape, F32),
        input_output_aliases={4: 0},
        compiler_params=params(16),
        cost_estimate=cost(1e9, 2 * MIB),
        name="put_half",
    )(place, where, received, latents, updated)


def exclusive_prefix(kept, other, where):
    half, width = kept.shape
    piece = jax.ShapeDtypeStruct((half // SIDE, width), BF16)
    pieces = vmem_call(chip_sum_kernel, "chip_sum", [piece] * SIDE, where, kept, other)
    sums = [pieces[0]] + [shift_tm(pieces[k], 0, k, 0) for k in range(1, SIDE)]
    row_sum = vmem_call(row_sum_kernel, "row_sum", [piece], where, *sums)[0]
    rows = [shift_tm(row_sum, k, 0, 0) for k in range(1, SIDE)]
    prefixes = vmem_call(prefix_kernel, "prefix", [piece] * SIDE, where, *sums, *rows)
    return [prefixes[0]] + [shift_tm(prefixes[k], 0, k, 0) for k in range(1, SIDE)]


def body(latents, noise, qkv_weight, qk_gains, out_weight, modulation, step_sizes, window_start):
    slot = lax.axis_index("tm")
    level = lax.axis_index("tensor")
    offset = window_start[0] + slot
    mod_row = lax.dynamic_index_in_dim(jnp.transpose(modulation, (1, 0, 2)), offset, 1, keepdims=False)
    step_size = lax.dynamic_index_in_dim(step_sizes, offset, 0, keepdims=False)
    own_rows = latents[0]
    length, width = own_rows.shape
    features = width * LEVELS
    half = length // 2
    at = lambda *offsets: jnp.stack([(level + k) % LEVELS for k in offsets]).astype(jnp.int32)

    aux = jnp.concatenate([mod_row[1:2], mod_row[0:1], jnp.zeros((AUX - 2, width), BF16)], axis=0)
    rounded = own_rows.astype(BF16)
    top, bottom = jnp.concatenate([rounded[:half], aux], axis=0), rounded[half:]
    core = slot % 2
    where = jnp.stack([slot // (2 * SIDE), slot // 2 % SIDE, core, slot // 2]).astype(jnp.int32)
    given_place, kept_place = (1 - core).reshape(1), core.reshape(1)
    other_rows = shift_tm(lax.dynamic_slice_in_dim(own_rows, (1 - core) * half, half, 0), 0, 0, 1)

    weight = jnp.transpose(qkv_weight, (1, 0, 2))
    up_top, up_bottom, down_top, down_bottom = top, bottom, top, bottom
    chunks, sources = [(top, bottom)], [0]
    for step in range(1, LEVELS // 2):
        up_top, down_bottom = shift_z(up_top, 1), shift_z(down_bottom, -1)
        up_bottom, down_top = shift_z(up_bottom, 1), shift_z(down_top, -1)
        chunks += [(up_top, up_bottom), (down_top, down_bottom)]
        sources += [-step, step]
    last = (shift_z(up_top, 1), shift_z(down_bottom, -1))
    state = project(chunks[:5], at(*sources[:5]), weight, None)
    state = project(chunks[5:], at(*sources[5:]), weight, state)
    query_scale = math.log2(math.e) / math.sqrt(HEAD)
    gains = jnp.stack([qk_gains[0] * query_scale, qk_gains[1]])
    qkv = finish(last, at(LEVELS // 2), weight, state, gains, features)

    far = LEVELS // 2
    scalars = jnp.stack([step_size, (slot == 0).astype(F32)])
    attended = [attend(qkv, given_place), attend(qkv, kept_place)]
    own, from_below, from_above = [None, None], [None, None], [None, None]
    for step in range(far):
        ahead = far - step
        for part in range(2):
            if step == 0:
                block, own[part] = partial(attended[part], out_weight, at(ahead, 0), [None, None])
                if part == 0:
                    from_below[0] = shift_z(block, 1)
                else:
                    from_above[1] = shift_z(block, -1)
                continue
            blocks = partial(attended[part], out_weight, at(ahead, -ahead), [from_below[part], from_above[part]])
            from_below[part], from_above[part] = shift_z(blocks[0], 1), shift_z(blocks[1], -1)
    gate = mod_row[2:3].astype(F32)
    velocity, given = update(
        given_place, scalars, own[0], (from_below[0], from_above[0]), gate, latents, noise, None
    )
    other = shift_tm(given, 0, 0, 1)
    velocity, kept = update(
        kept_place, scalars, own[1], (from_below[1], from_above[1]), gate, latents, noise, velocity
    )

    mine = exclusive_prefix(kept, other, where)
    updated, sent, squares = change(kept_place, where, mine, kept, other, latents, other_rows)
    updated = put_half(given_place, where, shift_tm(sent, 0, 0, 1), latents, updated)
    squares = lax.all_to_all(
        jnp.broadcast_to(squares, (LEVELS, *squares.shape)), "tensor", 0, 0, tiled=True
    )
    squares = jnp.sum(squares, axis=0)
    own_squares = jnp.where(core == 0, squares[:8], squares[8:])
    own_squares = own_squares + shift_tm(jnp.where(core == 0, squares[8:], squares[:8]), 0, 0, 1)
    slot_err = jnp.sum(own_squares) / (length * features)
    return updated, velocity, slot_err.reshape(1)


def solution(mesh):
    return jax.shard_map(
        body,
        mesh=mesh,
        in_specs=(
            P("tm", None, "tensor"),
            P("tm", None, "tensor"),
            P(None, None, "tensor"),
            P(None, "tensor"),
            P("tensor", None),
            P(None, None, "tensor"),
            P(),
            P(),
        ),
        out_specs=(P("tm", None, "tensor"), P("tm", None, "tensor"), P("tm")),
        check_vma=False,
    )
```

```python
import functools
import math

import jax
import jax.numpy as jnp
from jax import lax
from jax.experimental import pallas as pl
from jax.experimental.pallas import tpu as pltpu
from jax.sharding import PartitionSpec as P

HEAD = 128
LEVELS = 8
SIDE = 4
AUX = 16
epsilon = 1e-06
F32 = jnp.float32
BF16 = jnp.bfloat16
MIB = 1 << 20


def shift_z(value, step):
    return lax.ppermute(value, "tensor", [(i, (i + step) % LEVELS) for i in range(LEVELS)])


def tm_place(x, y, core):
    return (x % SIDE * SIDE + y % SIDE) * 2 + core


def shift_tm(value, dx, dy, swap):
    pairs = [
        (tm_place(x, y, c), tm_place(x + dx, y + dy, c ^ swap))
        for x in range(SIDE)
        for y in range(SIDE)
        for c in range(2)
    ]
    return lax.ppermute(value, "tm", pairs)


def params(mib):
    return pltpu.CompilerParams(vmem_limit_bytes=mib * MIB)


def cost(flops, moved):
    return pl.CostEstimate(flops=int(flops), bytes_accessed=int(moved), transcendentals=0)


def scale_chunk(top, bottom, scaled, column, s1_ref, s2_ref, fresh):
    half = bottom.shape[0] - AUX
    width = bottom.shape[1]
    lanes = pl.ds(column * width, width)
    aux = top[half : half + AUX, :].astype(F32)
    gain = 1.0 + aux[0:1]
    for part in range(2):
        piece = (top, bottom)[part]
        for block in range(half // 128):
            rows = pl.ds(part * half + block * 128, 128)
            x = piece[block * 128 : (block + 1) * 128, :].astype(F32)
            scaled[rows, lanes] = (x * gain).astype(BF16)
            square = x * x
            total, squares = x[:, :HEAD], square[:, :HEAD]
            for lane in range(HEAD, width, HEAD):
                total = total + x[:, lane : lane + HEAD]
                squares = squares + square[:, lane : lane + HEAD]
            if fresh:
                s1_ref[rows, :] = total
                s2_ref[rows, :] = squares
            else:
                s1_ref[rows, :] += total
                s2_ref[rows, :] += squares
    row = lax.broadcasted_iota(jnp.int32, (AUX, width), 0)
    high = gain.astype(BF16).astype(F32)
    extra = jnp.where(row == 0, high, jnp.where(row == 1, gain - high, jnp.where(row == 2, aux[1:2], 0.0)))
    scaled[pl.ds(2 * half, AUX), lanes] = extra.astype(BF16)


def project_kernel(count, has_state, sources, weight, *refs):
    refs = list(refs)
    chunks = [(refs[2 * i], refs[2 * i + 1]) for i in range(count)]
    refs = refs[2 * count :]
    if has_state:
        acc_in, s1_in, s2_in = refs[:3]
        refs = refs[3:]
    acc, s1, s2, scaled = refs
    width = weight.shape[2]
    if has_state:
        s1[...] = s1_in[...]
        s2[...] = s2_in[...]
    for i, (top, bottom) in enumerate(chunks):
        scale_chunk(top, bottom, scaled, i, s1, s2, not has_state and i == 0)
    starts = [pl.multiple_of(sources[i] * width, width) for i in range(count)]
    for j in range(3):
        rows = jnp.concatenate([weight[j, pl.ds(start, width), :] for start in starts], axis=0)
        total = jnp.dot(scaled[...], rows, preferred_element_type=F32)
        acc[j] = acc_in[j] + total if has_state else total


def whole_vmem(count):
    return [pl.BlockSpec(memory_space=pltpu.VMEM)] * count


SMEM = pl.BlockSpec(memory_space=pltpu.SMEM)
HBM = pl.BlockSpec(memory_space=pltpu.HBM)


def project(chunks, sources, weight, state, estimate):
    count = len(chunks)
    half, width = chunks[0][1].shape[0] - AUX, chunks[0][1].shape[1]
    rows = 2 * half + AUX
    operands = [weight] + [piece for chunk in chunks for piece in chunk]
    aliases = {}
    if state is not None:
        first = 1 + len(operands)
        aliases = {first: 0, first + 1: 1, first + 2: 2}
        operands += list(state)
    return pl.pallas_call(
        functools.partial(project_kernel, count, state is not None),
        in_specs=[pl.BlockSpec(memory_space=pltpu.SMEM)] + whole_vmem(len(operands)),
        out_specs=whole_vmem(3),
        scratch_shapes=[pltpu.VMEM((rows, count * width), BF16)],
        out_shape=[
            jax.ShapeDtypeStruct((3, rows, width), F32),
            jax.ShapeDtypeStruct((2 * half, HEAD), F32),
            jax.ShapeDtypeStruct((2 * half, HEAD), F32),
        ],
        input_output_aliases=aliases,
        compiler_params=params(16),
        cost_estimate=cost(estimate, 4 * MIB),
        name="project",
    )(sources, *operands)


def finish_kernel(features, sources, weight, top, bottom, acc_in, s1, s2, gains, out, scaled, sums):
    length, width = out.shape[1], out.shape[2]
    sums[0] = s1[...]
    sums[1] = s2[...]
    scale_chunk(top, bottom, scaled, 0, sums.at[0], sums.at[1], False)
    mean = jnp.sum(sums[0], axis=1, keepdims=True) * (1.0 / features)
    power = jnp.sum(sums[1], axis=1, keepdims=True) * (1.0 / features)
    rstd = lax.rsqrt(power - mean * mean + epsilon)
    source = pl.ds(pl.multiple_of(sources[0] * width, width), width)
    for j in range(3):
        total = acc_in[j] + jnp.dot(scaled[...], weight[j, source, :], preferred_element_type=F32)
        extra = total[length:, :]
        gain_product = extra[0:1] + extra[1:2]
        total = rstd * (total[:length, :] - mean * gain_product) + extra[2:3]
        for lane in range(0, width, HEAD):
            vectors = total[:, lane : lane + HEAD]
            if j < 2:
                square = jnp.mean(vectors * vectors, axis=1, keepdims=True)
                vectors = vectors * lax.rsqrt(square + epsilon) * gains[j : j + 1, lane : lane + HEAD]
            out[j, :, lane : lane + HEAD] = vectors.astype(BF16)


def finish(chunk, source, weight, state, gains, features):
    top, bottom = chunk
    half, width = bottom.shape[0] - AUX, bottom.shape[1]
    rows = 2 * half + AUX
    return pl.pallas_call(
        functools.partial(finish_kernel, features),
        in_specs=[pl.BlockSpec(memory_space=pltpu.SMEM)] + whole_vmem(7),
        out_specs=pl.BlockSpec(memory_space=pltpu.VMEM),
        scratch_shapes=[pltpu.VMEM((rows, width), BF16), pltpu.VMEM((2, 2 * half, HEAD), F32)],
        out_shape=jax.ShapeDtypeStruct((3, 2 * half, width), BF16),
        compiler_params=params(16),
        cost_estimate=cost(4e9, 4 * MIB),
        name="finish",
    )(source, weight, top, bottom, *state, gains)


def attend_kernel(place, qkv, out):
    tile = 256
    rows, width = out.shape
    for lane in range(0, width, HEAD):
        lanes = slice(lane, lane + HEAD)
        keys, values = qkv[1, :, lanes], qkv[2, :, lanes]
        for first in range(0, rows, tile):
            queries = qkv[0, pl.ds(pl.multiple_of(place[0] * rows + first, tile), tile), lanes]
            scores = lax.dot_general(queries, keys, (((1,), (1,)), ((), ())), preferred_element_type=F32)
            weights = jnp.exp2(scores - jnp.max(scores, axis=1, keepdims=True))
            total = jnp.sum(weights, axis=1, keepdims=True)
            mixed = jnp.dot(weights.astype(BF16), values, preferred_element_type=F32) / total
            out[first : first + tile, lanes] = mixed.astype(BF16)


def attend(qkv, place):
    _, length, width = qkv.shape
    return pl.pallas_call(
        attend_kernel,
        in_specs=[pl.BlockSpec(memory_space=pltpu.SMEM)] + whole_vmem(1),
        out_specs=pl.BlockSpec(memory_space=pltpu.VMEM),
        out_shape=jax.ShapeDtypeStruct((length // 2, width), BF16),
        compiler_params=params(16),
        cost_estimate=cost(4e9, 3 * MIB),
        name="attend",
    )(place, qkv)


def begin_kernel(offset, latents, modulation, top, bottom, gate):
    half, width = top.shape[0] - AUX, top.shape[1]
    top[:half, :] = latents[0, :half, :].astype(BF16)
    bottom[:half, :] = latents[0, half:, :].astype(BF16)
    steps = modulation.shape[1]
    chosen = lax.broadcasted_iota(jnp.int32, (steps, width), 0) == offset[0]
    pick = lambda i: jnp.sum(jnp.where(chosen, modulation[i].astype(F32), 0.0), axis=0, keepdims=True)
    row = lax.broadcasted_iota(jnp.int32, (AUX, width), 0)
    aux = jnp.where(row == 0, pick(1), jnp.where(row == 1, pick(0), 0.0)).astype(BF16)
    top[half:, :] = aux
    bottom[half:, :] = aux
    gate[...] = jnp.broadcast_to(pick(2), gate.shape)


def begin(offset, latents, modulation):
    _, length, width = latents.shape
    piece = jax.ShapeDtypeStruct((length // 2 + AUX, width), BF16)
    return pl.pallas_call(
        begin_kernel,
        in_specs=[SMEM] + whole_vmem(2),
        out_specs=whole_vmem(3),
        out_shape=[piece, piece, jax.ShapeDtypeStruct((8, width), F32)],
        compiler_params=params(16),
        cost_estimate=cost(1e9, 2 * MIB),
        name="begin",
    )(offset, latents, modulation)


def partial_kernel(has_sum, dest, attended, weight, *refs):
    count = len(has_sum)
    width = attended.shape[1]
    sums, outs = refs[:-count], refs[-count:]
    place = 0
    for i in range(count):
        columns = pl.ds(pl.multiple_of(dest[i] * width, width), width)
        total = jnp.dot(attended[...], weight[:, columns], preferred_element_type=F32)
        if has_sum[i]:
            total = total + sums[place][...].astype(F32)
            place += 1
        outs[i][...] = total.astype(BF16)


def partial(attended, weight, dest, sums):
    rows, width = attended.shape
    has_sum = [value is not None for value in sums]
    given = [value for value in sums if value is not None]
    return pl.pallas_call(
        functools.partial(partial_kernel, has_sum),
        in_specs=[pl.BlockSpec(memory_space=pltpu.SMEM)] + whole_vmem(2 + len(given)),
        out_specs=whole_vmem(len(sums)),
        out_shape=[jax.ShapeDtypeStruct((rows, width), BF16)] * len(sums),
        compiler_params=params(16),
        cost_estimate=cost(1e9, 2 * MIB),
        name="partial",
    )(dest, attended, weight, *given)


def update_kernel(places, scalars, own, from_below, from_above, gate, latents, noise, *refs):
    velocity_out, increment_out, x, noise_rows, arrived = refs[-5:]
    rows = own.shape[0]
    held = pl.ds(pl.multiple_of(places[0] * rows, rows), rows)
    copies = [
        pltpu.make_async_copy(latents.at[0, held, :], x, arrived.at[0]),
        pltpu.make_async_copy(noise.at[0, held, :], noise_rows, arrived.at[1]),
    ]
    for copy in copies:
        copy.start()
    branch = own[...].astype(F32) + from_below[...].astype(F32) + from_above[...].astype(F32)
    branch = gate[0:1, :] * branch
    for copy in copies:
        copy.wait()
    velocity = x[...] + branch
    velocity_out[0] = velocity.astype(BF16)
    increment = scalars[1] * x[...] - scalars[0] * velocity + noise_rows[...].astype(F32)
    increment_out[...] = increment.astype(BF16)


def update(place, scalars, own, sums, gate, latents, noise, velocity):
    rows, width = own.shape
    operands = [own, *sums, gate, latents, noise]
    in_specs = [SMEM] + whole_vmem(4) + [HBM, HBM]
    aliases = {}
    if velocity is not None:
        aliases = {2 + len(operands): 0}
        operands.append(velocity)
        in_specs.append(pl.BlockSpec(memory_space=pl.ANY))
    return pl.pallas_call(
        update_kernel,
        grid_spec=pltpu.PrefetchScalarGridSpec(
            num_scalar_prefetch=1,
            grid=(1,),
            in_specs=in_specs,
            out_specs=[pl.BlockSpec((1, rows, width), lambda i, p: (0, p[0], 0))] + whole_vmem(1),
            scratch_shapes=[
                pltpu.VMEM((rows, width), F32),
                pltpu.VMEM((rows, width), BF16),
                pltpu.SemaphoreType.DMA((2,)),
            ],
        ),
        out_shape=[
            jax.ShapeDtypeStruct((1, 2 * rows, width), BF16),
            jax.ShapeDtypeStruct((rows, width), BF16),
        ],
        input_output_aliases=aliases,
        compiler_params=params(16),
        cost_estimate=cost(1e9, 3 * MIB),
        name="update",
    )(place, scalars, *operands)


def vmem_call(kernel, name, out_shape, scalars, *operands):
    return pl.pallas_call(
        kernel,
        in_specs=[pl.BlockSpec(memory_space=pltpu.SMEM)] + whole_vmem(len(operands)),
        out_specs=whole_vmem(len(out_shape)),
        out_shape=out_shape,
        compiler_params=params(8),
        cost_estimate=cost(1e9, MIB),
        name=name,
    )(scalars, *operands)


def chip_sum_kernel(where, kept, other, *pieces):
    rows = pieces[0].shape[0]
    for k in range(SIDE):
        part = pl.ds(pl.multiple_of((where[1] + k) % SIDE * rows, rows), rows)
        pieces[k][...] = (kept[part, :].astype(F32) + other[part, :].astype(F32)).astype(BF16)


def row_sum_kernel(where, *refs):
    total = refs[0][...].astype(F32)
    for ref in refs[1:-1]:
        total = total + ref[...].astype(F32)
    refs[-1][...] = total.astype(BF16)


def prefix_kernel(where, *refs):
    x, y = where[0], where[1]
    sums = [ref[...].astype(F32) for ref in refs[:SIDE]]
    before = jnp.zeros_like(sums[0])
    for k in range(1, SIDE):
        before = before + jnp.where(x >= k, refs[SIDE + k - 1][...].astype(F32), 0.0)
    outs = refs[2 * SIDE - 1 :]
    for k in range(SIDE):
        total = before
        for source in range(SIDE):
            total = total + jnp.where((y + SIDE - source) % SIDE < (y + k) % SIDE, sums[source], 0.0)
        outs[k][...] = total.astype(BF16)


def square_sums(change):
    rows, width = change.shape
    square = jnp.sum((change * change).reshape(rows // 8, 8, width), axis=0)
    total = square[:, :HEAD]
    for lane in range(HEAD, width, HEAD):
        total = total + square[:, lane : lane + HEAD]
    return total


def change_kernel(places, where, *refs):
    mine, (kept, other, x) = refs[:SIDE], refs[SIDE : SIDE + 3]
    updated, sent, squares = refs[SIDE + 3 :]
    rows = mine[0].shape[0]
    y, first_core, first_chip = where[1], where[2] == 0, where[3] == 0
    total = jnp.zeros((8, HEAD), F32)
    for k in range(SIDE):
        part = pl.ds(pl.multiple_of((y + SIDE - k) % SIDE * rows, rows), rows)
        even = mine[k][...].astype(F32)
        odd = even + jnp.where(first_core, kept[part, :], other[part, :]).astype(F32)
        sent[part, :] = jnp.where(first_core, odd, even).astype(BF16)
        own_x = x[0, part, :]
        own = jnp.where(first_core, jnp.where(first_chip, own_x, even), odd)
        updated[0, part, :] = own
        total = total + square_sums(own - own_x)
    squares[...] = total


def change(place, where, mine, kept, other, latents):
    half, width = kept.shape
    block = pl.BlockSpec((1, half, width), lambda i, p: (0, p[0], 0))
    return pl.pallas_call(
        change_kernel,
        grid_spec=pltpu.PrefetchScalarGridSpec(
            num_scalar_prefetch=1,
            grid=(1,),
            in_specs=[SMEM] + whole_vmem(SIDE + 2) + [block],
            out_specs=[block] + whole_vmem(2),
        ),
        out_shape=[
            jax.ShapeDtypeStruct((1, 2 * half, width), F32),
            jax.ShapeDtypeStruct((half, width), BF16),
            jax.ShapeDtypeStruct((8, HEAD), F32),
        ],
        compiler_params=params(16),
        cost_estimate=cost(1e9, 3 * MIB),
        name="change",
    )(place, where, *mine, kept, other, latents)


def put_half_kernel(places, where, received, squares, x, _, updated, totals):
    first = jnp.logical_and(where[2] == 0, where[3] == 0)
    own = jnp.where(first, x[0], received[...].astype(F32))
    updated[0] = own
    total = squares[...] + square_sums(own - x[0])
    for level in range(LEVELS):
        totals[level] = total


def put_half(place, where, received, squares, latents, updated):
    half, width = received.shape
    block = pl.BlockSpec((1, half, width), lambda i, p: (0, p[0], 0))
    return pl.pallas_call(
        put_half_kernel,
        grid_spec=pltpu.PrefetchScalarGridSpec(
            num_scalar_prefetch=1,
            grid=(1,),
            in_specs=[SMEM] + whole_vmem(2) + [block, pl.BlockSpec(memory_space=pl.ANY)],
            out_specs=[block] + whole_vmem(1),
        ),
        out_shape=[
            jax.ShapeDtypeStruct(updated.shape, F32),
            jax.ShapeDtypeStruct((LEVELS, 8, HEAD), F32),
        ],
        input_output_aliases={5: 0},
        compiler_params=params(16),
        cost_estimate=cost(1e9, 2 * MIB),
        name="put_half",
    )(place, where, received, squares, latents, updated)


def exclusive_prefix(kept, other, where):
    half, width = kept.shape
    piece = jax.ShapeDtypeStruct((half // SIDE, width), BF16)
    pieces = vmem_call(chip_sum_kernel, "chip_sum", [piece] * SIDE, where, kept, other)
    sums = [pieces[0]] + [shift_tm(pieces[k], 0, k, 0) for k in range(1, SIDE)]
    row_sum = vmem_call(row_sum_kernel, "row_sum", [piece], where, *sums)[0]
    rows = [shift_tm(row_sum, k, 0, 0) for k in range(1, SIDE)]
    prefixes = vmem_call(prefix_kernel, "prefix", [piece] * SIDE, where, *sums, *rows)
    return [prefixes[0]] + [shift_tm(prefixes[k], 0, k, 0) for k in range(1, SIDE)]


def body(latents, noise, qkv_weight, qk_gains, out_weight, modulation, step_sizes, window_start):
    slot = lax.axis_index("tm")
    level = lax.axis_index("tensor")
    offset = window_start[0] + slot
    step_size = lax.dynamic_index_in_dim(step_sizes, offset, 0, keepdims=False)
    own_rows = latents[0]
    length, width = own_rows.shape
    features = width * LEVELS
    half = length // 2
    at = lambda *offsets: jnp.stack([(level + k) % LEVELS for k in offsets]).astype(jnp.int32)

    top, bottom, gate = begin(offset.reshape(1), latents, jnp.transpose(modulation, (1, 0, 2)))
    core = slot % 2
    where = jnp.stack([slot // (2 * SIDE), slot // 2 % SIDE, core, slot // 2]).astype(jnp.int32)
    given_place, kept_place = (1 - core).reshape(1), core.reshape(1)

    weight = jnp.transpose(qkv_weight, (1, 0, 2))
    up_top, up_bottom, down_top, down_bottom = top, bottom, top, bottom
    state = project([(top, bottom)], at(0), weight, None, 40e9)
    for step in range(1, LEVELS // 2):
        up_top, down_top = shift_z(up_top, 1), shift_z(down_top, -1)
        up_bottom, down_bottom = shift_z(up_bottom, 1), shift_z(down_bottom, -1)
        state = project([(up_top, up_bottom), (down_top, down_bottom)], at(-step, step), weight, state, 40e9)
    last = (shift_z(up_top, 1), shift_z(down_bottom, -1))
    query_scale = math.log2(math.e) / math.sqrt(HEAD)
    gains = jnp.stack([qk_gains[0] * query_scale, qk_gains[1]])
    qkv = finish(last, at(LEVELS // 2), weight, state, gains, features)

    far = LEVELS // 2
    scalars = jnp.stack([step_size, (slot == 0).astype(F32)])
    attended = [attend(qkv, given_place), attend(qkv, kept_place)]
    own, from_below, from_above = [None, None], [None, None], [None, None]
    for step in range(far):
        ahead = far - step
        for part in range(2):
            if step == 0:
                block, own[part] = partial(attended[part], out_weight, at(ahead, 0), [None, None])
                if part == 0:
                    from_below[0] = shift_z(block, 1)
                else:
                    from_above[1] = shift_z(block, -1)
                continue
            blocks = partial(attended[part], out_weight, at(ahead, -ahead), [from_below[part], from_above[part]])
            from_below[part], from_above[part] = shift_z(blocks[0], 1), shift_z(blocks[1], -1)
    velocity, given = update(
        given_place, scalars, own[0], (from_below[0], from_above[0]), gate, latents, noise, None
    )
    other = shift_tm(given, 0, 0, 1)
    velocity, kept = update(
        kept_place, scalars, own[1], (from_below[1], from_above[1]), gate, latents, noise, velocity
    )

    mine = exclusive_prefix(kept, other, where)
    updated, sent, squares = change(kept_place, where, mine, kept, other, latents)
    updated, squares = put_half(given_place, where, shift_tm(sent, 0, 0, 1), squares, latents, updated)
    squares = lax.all_to_all(squares, "tensor", 0, 0, tiled=True)
    slot_err = jnp.sum(squares) / (length * features)
    return updated, velocity, slot_err.reshape(1)


def solution(mesh):
    return jax.shard_map(
        body,
        mesh=mesh,
        in_specs=(
            P("tm", None, "tensor"),
            P("tm", None, "tensor"),
            P(None, None, "tensor"),
            P(None, "tensor"),
            P("tensor", None),
            P(None, None, "tensor"),
            P(),
            P(),
        ),
        out_specs=(P("tm", None, "tensor"), P("tm", None, "tensor"), P("tm")),
        check_vma=False,
    )
```

```python
import functools
import math

import jax
import jax.numpy as jnp
from jax import lax
from jax.experimental import pallas as pl
from jax.experimental.pallas import tpu as pltpu
from jax.sharding import PartitionSpec as P

HEAD = 128
LEVELS = 8
SIDE = 4
AUX = 16
epsilon = 1e-06
F32 = jnp.float32
BF16 = jnp.bfloat16
MIB = 1 << 20


def shift_z(value, step):
    return lax.ppermute(value, "tensor", [(i, (i + step) % LEVELS) for i in range(LEVELS)])


def tm_place(x, y, core):
    return (x % SIDE * SIDE + y % SIDE) * 2 + core


def shift_tm(value, dx, dy, swap):
    pairs = [
        (tm_place(x, y, c), tm_place(x + dx, y + dy, c ^ swap))
        for x in range(SIDE)
        for y in range(SIDE)
        for c in range(2)
    ]
    return lax.ppermute(value, "tm", pairs)


def params(mib):
    return pltpu.CompilerParams(vmem_limit_bytes=mib * MIB)


def cost(flops, moved):
    return pl.CostEstimate(flops=int(flops), bytes_accessed=int(moved), transcendentals=0)


def scale_chunk(top, bottom, scaled, column, s1_ref, s2_ref, fresh):
    half = bottom.shape[0] - AUX
    width = bottom.shape[1]
    lanes = pl.ds(column * width, width)
    aux = top[half : half + AUX, :].astype(F32)
    gain = 1.0 + aux[0:1]
    for part in range(2):
        piece = (top, bottom)[part]
        for block in range(half // 128):
            rows = pl.ds(part * half + block * 128, 128)
            x = piece[block * 128 : (block + 1) * 128, :].astype(F32)
            scaled[rows, lanes] = (x * gain).astype(BF16)
            square = x * x
            total, squares = x[:, :HEAD], square[:, :HEAD]
            for lane in range(HEAD, width, HEAD):
                total = total + x[:, lane : lane + HEAD]
                squares = squares + square[:, lane : lane + HEAD]
            if fresh:
                s1_ref[rows, :] = total
                s2_ref[rows, :] = squares
            else:
                s1_ref[rows, :] += total
                s2_ref[rows, :] += squares
    row = lax.broadcasted_iota(jnp.int32, (AUX, width), 0)
    high = gain.astype(BF16).astype(F32)
    extra = jnp.where(row == 0, high, jnp.where(row == 1, gain - high, jnp.where(row == 2, aux[1:2], 0.0)))
    scaled[pl.ds(2 * half, AUX), lanes] = extra.astype(BF16)


def project_kernel(count, has_state, sources, weight, *refs):
    refs = list(refs)
    chunks = [(refs[2 * i], refs[2 * i + 1]) for i in range(count)]
    refs = refs[2 * count :]
    if has_state:
        acc_in, s1_in, s2_in = refs[:3]
        refs = refs[3:]
    acc, s1, s2, scaled = refs
    width = weight.shape[2]
    if has_state:
        s1[...] = s1_in[...]
        s2[...] = s2_in[...]
    for i, (top, bottom) in enumerate(chunks):
        scale_chunk(top, bottom, scaled, i, s1, s2, not has_state and i == 0)
    starts = [pl.multiple_of(sources[i] * width, width) for i in range(count)]
    for j in range(3):
        rows = jnp.concatenate([weight[j, pl.ds(start, width), :] for start in starts], axis=0)
        total = jnp.dot(scaled[...], rows, preferred_element_type=F32)
        acc[j] = acc_in[j] + total if has_state else total


def whole_vmem(count):
    return [pl.BlockSpec(memory_space=pltpu.VMEM)] * count


SMEM = pl.BlockSpec(memory_space=pltpu.SMEM)
HBM = pl.BlockSpec(memory_space=pltpu.HBM)


def project(chunks, sources, weight, state, estimate):
    count = len(chunks)
    half, width = chunks[0][1].shape[0] - AUX, chunks[0][1].shape[1]
    rows = 2 * half + AUX
    operands = [weight] + [piece for chunk in chunks for piece in chunk]
    aliases = {}
    if state is not None:
        first = 1 + len(operands)
        aliases = {first: 0, first + 1: 1, first + 2: 2}
        operands += list(state)
    return pl.pallas_call(
        functools.partial(project_kernel, count, state is not None),
        in_specs=[pl.BlockSpec(memory_space=pltpu.SMEM)] + whole_vmem(len(operands)),
        out_specs=whole_vmem(3),
        scratch_shapes=[pltpu.VMEM((rows, count * width), BF16)],
        out_shape=[
            jax.ShapeDtypeStruct((3, rows, width), F32),
            jax.ShapeDtypeStruct((2 * half, HEAD), F32),
            jax.ShapeDtypeStruct((2 * half, HEAD), F32),
        ],
        input_output_aliases=aliases,
        compiler_params=params(16),
        cost_estimate=cost(estimate, 4 * MIB),
        name="project",
    )(sources, *operands)


def finish_kernel(features, sources, weight, top, bottom, acc_in, s1, s2, gains, out, scaled, sums):
    length, width = out.shape[1], out.shape[2]
    sums[0] = s1[...]
    sums[1] = s2[...]
    scale_chunk(top, bottom, scaled, 0, sums.at[0], sums.at[1], False)
    mean = jnp.sum(sums[0], axis=1, keepdims=True) * (1.0 / features)
    power = jnp.sum(sums[1], axis=1, keepdims=True) * (1.0 / features)
    rstd = lax.rsqrt(power - mean * mean + epsilon)
    source = pl.ds(pl.multiple_of(sources[0] * width, width), width)
    for j in range(3):
        total = acc_in[j] + jnp.dot(scaled[...], weight[j, source, :], preferred_element_type=F32)
        extra = total[length:, :]
        gain_product = extra[0:1] + extra[1:2]
        total = rstd * (total[:length, :] - mean * gain_product) + extra[2:3]
        for lane in range(0, width, HEAD):
            vectors = total[:, lane : lane + HEAD]
            if j < 2:
                square = jnp.mean(vectors * vectors, axis=1, keepdims=True)
                vectors = vectors * lax.rsqrt(square + epsilon) * gains[j : j + 1, lane : lane + HEAD]
            out[j, :, lane : lane + HEAD] = vectors.astype(BF16)


def finish(chunk, source, weight, state, gains, features):
    top, bottom = chunk
    half, width = bottom.shape[0] - AUX, bottom.shape[1]
    rows = 2 * half + AUX
    return pl.pallas_call(
        functools.partial(finish_kernel, features),
        in_specs=[pl.BlockSpec(memory_space=pltpu.SMEM)] + whole_vmem(7),
        out_specs=pl.BlockSpec(memory_space=pltpu.VMEM),
        scratch_shapes=[pltpu.VMEM((rows, width), BF16), pltpu.VMEM((2, 2 * half, HEAD), F32)],
        out_shape=jax.ShapeDtypeStruct((3, 2 * half, width), BF16),
        compiler_params=params(16),
        cost_estimate=cost(4e9, 4 * MIB),
        name="finish",
    )(source, weight, top, bottom, *state, gains)


def attend_kernel(place, qkv, out):
    tile = 256
    rows, width = out.shape
    for lane in range(0, width, HEAD):
        lanes = slice(lane, lane + HEAD)
        keys, values = qkv[1, :, lanes], qkv[2, :, lanes]
        for first in range(0, rows, tile):
            queries = qkv[0, pl.ds(pl.multiple_of(place[0] * rows + first, tile), tile), lanes]
            scores = lax.dot_general(queries, keys, (((1,), (1,)), ((), ())), preferred_element_type=F32)
            weights = jnp.exp2(scores - jnp.max(scores, axis=1, keepdims=True))
            total = jnp.sum(weights, axis=1, keepdims=True)
            mixed = jnp.dot(weights.astype(BF16), values, preferred_element_type=F32) / total
            out[first : first + tile, lanes] = mixed.astype(BF16)


def attend(qkv, place):
    _, length, width = qkv.shape
    return pl.pallas_call(
        attend_kernel,
        in_specs=[pl.BlockSpec(memory_space=pltpu.SMEM)] + whole_vmem(1),
        out_specs=pl.BlockSpec(memory_space=pltpu.VMEM),
        out_shape=jax.ShapeDtypeStruct((length // 2, width), BF16),
        compiler_params=params(16),
        cost_estimate=cost(4e9, 3 * MIB),
        name="attend",
    )(place, qkv)


def begin_kernel(offset, latents, modulation, top, bottom, gate):
    half, width = top.shape[0] - AUX, top.shape[1]
    top[:half, :] = latents[0, :half, :].astype(BF16)
    bottom[:half, :] = latents[0, half:, :].astype(BF16)
    steps = modulation.shape[1]
    chosen = lax.broadcasted_iota(jnp.int32, (steps, width), 0) == offset[0]
    pick = lambda i: jnp.sum(jnp.where(chosen, modulation[i].astype(F32), 0.0), axis=0, keepdims=True)
    row = lax.broadcasted_iota(jnp.int32, (AUX, width), 0)
    aux = jnp.where(row == 0, pick(1), jnp.where(row == 1, pick(0), 0.0)).astype(BF16)
    top[half:, :] = aux
    bottom[half:, :] = aux
    gate[...] = jnp.broadcast_to(pick(2), gate.shape)


def begin(offset, latents, modulation):
    _, length, width = latents.shape
    piece = jax.ShapeDtypeStruct((length // 2 + AUX, width), BF16)
    return pl.pallas_call(
        begin_kernel,
        in_specs=[SMEM] + whole_vmem(2),
        out_specs=whole_vmem(3),
        out_shape=[piece, piece, jax.ShapeDtypeStruct((8, width), F32)],
        compiler_params=params(16),
        cost_estimate=cost(1e9, 2 * MIB),
        name="begin",
    )(offset, latents, modulation)


def partial_kernel(has_sum, dest, attended, weight, *refs):
    count = len(has_sum)
    width = attended.shape[1]
    sums, outs = refs[:-count], refs[-count:]
    place = 0
    for i in range(count):
        columns = pl.ds(pl.multiple_of(dest[i] * width, width), width)
        total = jnp.dot(attended[...], weight[:, columns], preferred_element_type=F32)
        if has_sum[i]:
            total = total + sums[place][...].astype(F32)
            place += 1
        outs[i][...] = total.astype(BF16)


def partial(attended, weight, dest, sums):
    rows, width = attended.shape
    has_sum = [value is not None for value in sums]
    given = [value for value in sums if value is not None]
    return pl.pallas_call(
        functools.partial(partial_kernel, has_sum),
        in_specs=[pl.BlockSpec(memory_space=pltpu.SMEM)] + whole_vmem(2 + len(given)),
        out_specs=whole_vmem(len(sums)),
        out_shape=[jax.ShapeDtypeStruct((rows, width), BF16)] * len(sums),
        compiler_params=params(16),
        cost_estimate=cost(8e9, 2 * MIB),
        name="partial",
    )(dest, attended, weight, *given)


def update_kernel(places, scalars, own, from_below, from_above, gate, latents, noise, *refs):
    velocity_out, increment_out, x, noise_rows, arrived = refs[-5:]
    rows = own.shape[0]
    held = pl.ds(pl.multiple_of(places[0] * rows, rows), rows)
    copies = [
        pltpu.make_async_copy(latents.at[0, held, :], x, arrived.at[0]),
        pltpu.make_async_copy(noise.at[0, held, :], noise_rows, arrived.at[1]),
    ]
    for copy in copies:
        copy.start()
    branch = own[...].astype(F32) + from_below[...].astype(F32) + from_above[...].astype(F32)
    branch = gate[0:1, :] * branch
    for copy in copies:
        copy.wait()
    velocity = x[...] + branch
    velocity_out[0] = velocity.astype(BF16)
    increment = scalars[1] * x[...] - scalars[0] * velocity + noise_rows[...].astype(F32)
    increment_out[...] = increment.astype(BF16)


def update(place, scalars, own, sums, gate, latents, noise, velocity):
    rows, width = own.shape
    operands = [own, *sums, gate, latents, noise]
    in_specs = [SMEM] + whole_vmem(4) + [HBM, HBM]
    aliases = {}
    if velocity is not None:
        aliases = {2 + len(operands): 0}
        operands.append(velocity)
        in_specs.append(pl.BlockSpec(memory_space=pl.ANY))
    return pl.pallas_call(
        update_kernel,
        grid_spec=pltpu.PrefetchScalarGridSpec(
            num_scalar_prefetch=1,
            grid=(1,),
            in_specs=in_specs,
            out_specs=[pl.BlockSpec((1, rows, width), lambda i, p: (0, p[0], 0))] + whole_vmem(1),
            scratch_shapes=[
                pltpu.VMEM((rows, width), F32),
                pltpu.VMEM((rows, width), BF16),
                pltpu.SemaphoreType.DMA((2,)),
            ],
        ),
        out_shape=[
            jax.ShapeDtypeStruct((1, 2 * rows, width), BF16),
            jax.ShapeDtypeStruct((rows, width), BF16),
        ],
        input_output_aliases=aliases,
        compiler_params=params(16),
        cost_estimate=cost(1e9, 3 * MIB),
        name="update",
    )(place, scalars, *operands)


def vmem_call(kernel, name, out_shape, scalars, *operands):
    return pl.pallas_call(
        kernel,
        in_specs=[pl.BlockSpec(memory_space=pltpu.SMEM)] + whole_vmem(len(operands)),
        out_specs=whole_vmem(len(out_shape)),
        out_shape=out_shape,
        compiler_params=params(8),
        cost_estimate=cost(1e9, MIB),
        name=name,
    )(scalars, *operands)


def chip_sum_kernel(where, kept, other, *pieces):
    rows = pieces[0].shape[0]
    for k in range(SIDE):
        part = pl.ds(pl.multiple_of((where[1] + k) % SIDE * rows, rows), rows)
        pieces[k][...] = (kept[part, :].astype(F32) + other[part, :].astype(F32)).astype(BF16)


def row_sum_kernel(where, *refs):
    total = refs[0][...].astype(F32)
    for ref in refs[1:-1]:
        total = total + ref[...].astype(F32)
    refs[-1][...] = total.astype(BF16)


def prefix_kernel(where, *refs):
    x, y = where[0], where[1]
    sums = [ref[...].astype(F32) for ref in refs[:SIDE]]
    before = jnp.zeros_like(sums[0])
    for k in range(1, SIDE):
        before = before + jnp.where(x >= k, refs[SIDE + k - 1][...].astype(F32), 0.0)
    outs = refs[2 * SIDE - 1 :]
    for k in range(SIDE):
        total = before
        for source in range(SIDE):
            total = total + jnp.where((y + SIDE - source) % SIDE < (y + k) % SIDE, sums[source], 0.0)
        outs[k][...] = total.astype(BF16)


def square_sums(change):
    rows, width = change.shape
    square = jnp.sum((change * change).reshape(rows // 8, 8, width), axis=0)
    total = square[:, :HEAD]
    for lane in range(HEAD, width, HEAD):
        total = total + square[:, lane : lane + HEAD]
    return total


def change_kernel(places, where, *refs):
    mine, (kept, other, x) = refs[:SIDE], refs[SIDE : SIDE + 3]
    updated, sent, squares = refs[SIDE + 3 :]
    rows = mine[0].shape[0]
    y, first_core, first_chip = where[1], where[2] == 0, where[3] == 0
    total = jnp.zeros((8, HEAD), F32)
    for k in range(SIDE):
        part = pl.ds(pl.multiple_of((y + SIDE - k) % SIDE * rows, rows), rows)
        even = mine[k][...].astype(F32)
        odd = even + jnp.where(first_core, kept[part, :], other[part, :]).astype(F32)
        sent[part, :] = jnp.where(first_core, odd, even).astype(BF16)
        own_x = x[0, part, :]
        own = jnp.where(first_core, jnp.where(first_chip, own_x, even), odd)
        updated[0, part, :] = own
        total = total + square_sums(own - own_x)
    squares[...] = total


def change(place, where, mine, kept, other, latents):
    half, width = kept.shape
    block = pl.BlockSpec((1, half, width), lambda i, p: (0, p[0], 0))
    return pl.pallas_call(
        change_kernel,
        grid_spec=pltpu.PrefetchScalarGridSpec(
            num_scalar_prefetch=1,
            grid=(1,),
            in_specs=[SMEM] + whole_vmem(SIDE + 2) + [block],
            out_specs=[block] + whole_vmem(2),
        ),
        out_shape=[
            jax.ShapeDtypeStruct((1, 2 * half, width), F32),
            jax.ShapeDtypeStruct((half, width), BF16),
            jax.ShapeDtypeStruct((8, HEAD), F32),
        ],
        compiler_params=params(16),
        cost_estimate=cost(1e9, 3 * MIB),
        name="change",
    )(place, where, *mine, kept, other, latents)


def put_half_kernel(places, where, received, squares, x, _, updated, totals):
    first = jnp.logical_and(where[2] == 0, where[3] == 0)
    own = jnp.where(first, x[0], received[...].astype(F32))
    updated[0] = own
    total = squares[...] + square_sums(own - x[0])
    for level in range(LEVELS):
        totals[level] = total


def put_half(place, where, received, squares, latents, updated):
    half, width = received.shape
    block = pl.BlockSpec((1, half, width), lambda i, p: (0, p[0], 0))
    return pl.pallas_call(
        put_half_kernel,
        grid_spec=pltpu.PrefetchScalarGridSpec(
            num_scalar_prefetch=1,
            grid=(1,),
            in_specs=[SMEM] + whole_vmem(2) + [block, pl.BlockSpec(memory_space=pl.ANY)],
            out_specs=[block] + whole_vmem(1),
        ),
        out_shape=[
            jax.ShapeDtypeStruct(updated.shape, F32),
            jax.ShapeDtypeStruct((LEVELS, 8, HEAD), F32),
        ],
        input_output_aliases={5: 0},
        compiler_params=params(16),
        cost_estimate=cost(1e9, 2 * MIB),
        name="put_half",
    )(place, where, received, squares, latents, updated)


def exclusive_prefix(kept, other, where):
    half, width = kept.shape
    piece = jax.ShapeDtypeStruct((half // SIDE, width), BF16)
    pieces = vmem_call(chip_sum_kernel, "chip_sum", [piece] * SIDE, where, kept, other)
    sums = [pieces[0]] + [shift_tm(pieces[k], 0, k, 0) for k in range(1, SIDE)]
    row_sum = vmem_call(row_sum_kernel, "row_sum", [piece], where, *sums)[0]
    rows = [shift_tm(row_sum, k, 0, 0) for k in range(1, SIDE)]
    prefixes = vmem_call(prefix_kernel, "prefix", [piece] * SIDE, where, *sums, *rows)
    return [prefixes[0]] + [shift_tm(prefixes[k], 0, k, 0) for k in range(1, SIDE)]


def body(latents, noise, qkv_weight, qk_gains, out_weight, modulation, step_sizes, window_start):
    slot = lax.axis_index("tm")
    level = lax.axis_index("tensor")
    offset = window_start[0] + slot
    step_size = lax.dynamic_index_in_dim(step_sizes, offset, 0, keepdims=False)
    own_rows = latents[0]
    length, width = own_rows.shape
    features = width * LEVELS
    half = length // 2
    at = lambda *offsets: jnp.stack([(level + k) % LEVELS for k in offsets]).astype(jnp.int32)

    top, bottom, gate = begin(offset.reshape(1), latents, jnp.transpose(modulation, (1, 0, 2)))
    core = slot % 2
    where = jnp.stack([slot // (2 * SIDE), slot // 2 % SIDE, core, slot // 2]).astype(jnp.int32)
    given_place, kept_place = (1 - core).reshape(1), core.reshape(1)

    weight = jnp.transpose(qkv_weight, (1, 0, 2))
    up_top, up_bottom, down_top, down_bottom = top, bottom, top, bottom
    state = project([(top, bottom)], at(0), weight, None, 40e9)
    for step in range(1, LEVELS // 2):
        up_top, down_top = shift_z(up_top, 1), shift_z(down_top, -1)
        up_bottom, down_bottom = shift_z(up_bottom, 1), shift_z(down_bottom, -1)
        state = project([(up_top, up_bottom), (down_top, down_bottom)], at(-step, step), weight, state, 40e9)
    last = (shift_z(up_top, 1), shift_z(down_bottom, -1))
    query_scale = math.log2(math.e) / math.sqrt(HEAD)
    gains = jnp.stack([qk_gains[0] * query_scale, qk_gains[1]])
    qkv = finish(last, at(LEVELS // 2), weight, state, gains, features)

    far = LEVELS // 2
    scalars = jnp.stack([step_size, (slot == 0).astype(F32)])
    attended = [attend(qkv, given_place), attend(qkv, kept_place)]
    own, from_below, from_above = [None, None], [None, None], [None, None]
    for step in range(far):
        ahead = far - step
        for part in range(2):
            if step == 0:
                block, own[part] = partial(attended[part], out_weight, at(ahead, 0), [None, None])
                if part == 0:
                    from_below[0] = shift_z(block, 1)
                else:
                    from_above[1] = shift_z(block, -1)
                continue
            blocks = partial(attended[part], out_weight, at(ahead, -ahead), [from_below[part], from_above[part]])
            from_below[part], from_above[part] = shift_z(blocks[0], 1), shift_z(blocks[1], -1)
    velocity, given = update(
        given_place, scalars, own[0], (from_below[0], from_above[0]), gate, latents, noise, None
    )
    other = shift_tm(given, 0, 0, 1)
    velocity, kept = update(
        kept_place, scalars, own[1], (from_below[1], from_above[1]), gate, latents, noise, velocity
    )

    mine = exclusive_prefix(kept, other, where)
    updated, sent, squares = change(kept_place, where, mine, kept, other, latents)
    updated, squares = put_half(given_place, where, shift_tm(sent, 0, 0, 1), squares, latents, updated)
    squares = lax.all_to_all(squares, "tensor", 0, 0, tiled=True)
    slot_err = jnp.sum(squares) / (length * features)
    return updated, velocity, slot_err.reshape(1)


def solution(mesh):
    return jax.shard_map(
        body,
        mesh=mesh,
        in_specs=(
            P("tm", None, "tensor"),
            P("tm", None, "tensor"),
            P(None, None, "tensor"),
            P(None, "tensor"),
            P("tensor", None),
            P(None, None, "tensor"),
            P(),
            P(),
        ),
        out_specs=(P("tm", None, "tensor"), P("tm", None, "tensor"), P("tm")),
        check_vma=False,
    )
```

```python
import functools
import math

import jax
import jax.numpy as jnp
from jax import lax
from jax.experimental import pallas as pl
from jax.experimental.pallas import tpu as pltpu
from jax.sharding import PartitionSpec as P

HEAD = 128
LEVELS = 8
SIDE = 4
AUX = 16
epsilon = 1e-06
F32 = jnp.float32
BF16 = jnp.bfloat16
MIB = 1 << 20


def shift_z(value, step):
    return lax.ppermute(value, "tensor", [(i, (i + step) % LEVELS) for i in range(LEVELS)])


def tm_place(x, y, core):
    return (x % SIDE * SIDE + y % SIDE) * 2 + core


def shift_tm(value, dx, dy, swap):
    pairs = [
        (tm_place(x, y, c), tm_place(x + dx, y + dy, c ^ swap))
        for x in range(SIDE)
        for y in range(SIDE)
        for c in range(2)
    ]
    return lax.ppermute(value, "tm", pairs)


def params(mib):
    return pltpu.CompilerParams(vmem_limit_bytes=mib * MIB)


def cost(flops, moved):
    return pl.CostEstimate(flops=int(flops), bytes_accessed=int(moved), transcendentals=0)


def scale_chunk(top, bottom, scaled, column, s1_ref, s2_ref, fresh):
    half = bottom.shape[0] - AUX
    width = bottom.shape[1]
    lanes = pl.ds(column * width, width)
    aux = top[half : half + AUX, :].astype(F32)
    gain = 1.0 + aux[0:1]
    for part in range(2):
        piece = (top, bottom)[part]
        for block in range(half // 128):
            rows = pl.ds(part * half + block * 128, 128)
            x = piece[block * 128 : (block + 1) * 128, :].astype(F32)
            scaled[rows, lanes] = (x * gain).astype(BF16)
            square = x * x
            total, squares = x[:, :HEAD], square[:, :HEAD]
            for lane in range(HEAD, width, HEAD):
                total = total + x[:, lane : lane + HEAD]
                squares = squares + square[:, lane : lane + HEAD]
            if fresh:
                s1_ref[rows, :] = total
                s2_ref[rows, :] = squares
            else:
                s1_ref[rows, :] += total
                s2_ref[rows, :] += squares
    row = lax.broadcasted_iota(jnp.int32, (AUX, width), 0)
    high = gain.astype(BF16).astype(F32)
    extra = jnp.where(row == 0, high, jnp.where(row == 1, gain - high, jnp.where(row == 2, aux[1:2], 0.0)))
    scaled[pl.ds(2 * half, AUX), lanes] = extra.astype(BF16)


def project_kernel(count, has_state, sources, weight, *refs):
    refs = list(refs)
    chunks = [(refs[2 * i], refs[2 * i + 1]) for i in range(count)]
    refs = refs[2 * count :]
    if has_state:
        acc_in, s1_in, s2_in = refs[:3]
        refs = refs[3:]
    acc, s1, s2, scaled = refs
    width = weight.shape[2]
    if has_state:
        s1[...] = s1_in[...]
        s2[...] = s2_in[...]
    for i, (top, bottom) in enumerate(chunks):
        scale_chunk(top, bottom, scaled, i, s1, s2, not has_state and i == 0)
    starts = [pl.multiple_of(sources[i] * width, width) for i in range(count)]
    for j in range(3):
        rows = jnp.concatenate([weight[j, pl.ds(start, width), :] for start in starts], axis=0)
        total = jnp.dot(scaled[...], rows, preferred_element_type=F32)
        acc[j] = acc_in[j] + total if has_state else total


def whole_vmem(count):
    return [pl.BlockSpec(memory_space=pltpu.VMEM)] * count


SMEM = pl.BlockSpec(memory_space=pltpu.SMEM)
HBM = pl.BlockSpec(memory_space=pltpu.HBM)


def project(chunks, sources, weight, state, estimate):
    count = len(chunks)
    half, width = chunks[0][1].shape[0] - AUX, chunks[0][1].shape[1]
    rows = 2 * half + AUX
    operands = [weight] + [piece for chunk in chunks for piece in chunk]
    aliases = {}
    if state is not None:
        first = 1 + len(operands)
        aliases = {first: 0, first + 1: 1, first + 2: 2}
        operands += list(state)
    return pl.pallas_call(
        functools.partial(project_kernel, count, state is not None),
        in_specs=[pl.BlockSpec(memory_space=pltpu.SMEM)] + whole_vmem(len(operands)),
        out_specs=whole_vmem(3),
        scratch_shapes=[pltpu.VMEM((rows, count * width), BF16)],
        out_shape=[
            jax.ShapeDtypeStruct((3, rows, width), F32),
            jax.ShapeDtypeStruct((2 * half, HEAD), F32),
            jax.ShapeDtypeStruct((2 * half, HEAD), F32),
        ],
        input_output_aliases=aliases,
        compiler_params=params(16),
        cost_estimate=cost(estimate, 4 * MIB),
        name="project",
    )(sources, *operands)


def finish_kernel(features, sources, weight, top, bottom, acc_in, s1, s2, gains, out, scaled, sums):
    length, width = out.shape[1], out.shape[2]
    sums[0] = s1[...]
    sums[1] = s2[...]
    scale_chunk(top, bottom, scaled, 0, sums.at[0], sums.at[1], False)
    mean = jnp.sum(sums[0], axis=1, keepdims=True) * (1.0 / features)
    power = jnp.sum(sums[1], axis=1, keepdims=True) * (1.0 / features)
    rstd = lax.rsqrt(power - mean * mean + epsilon)
    source = pl.ds(pl.multiple_of(sources[0] * width, width), width)
    for j in range(3):
        total = acc_in[j] + jnp.dot(scaled[...], weight[j, source, :], preferred_element_type=F32)
        extra = total[length:, :]
        gain_product = extra[0:1] + extra[1:2]
        total = rstd * (total[:length, :] - mean * gain_product) + extra[2:3]
        for lane in range(0, width, HEAD):
            vectors = total[:, lane : lane + HEAD]
            if j < 2:
                square = jnp.mean(vectors * vectors, axis=1, keepdims=True)
                vectors = vectors * lax.rsqrt(square + epsilon) * gains[j : j + 1, lane : lane + HEAD]
            out[j, :, lane : lane + HEAD] = vectors.astype(BF16)


def finish(chunk, source, weight, state, gains, features):
    top, bottom = chunk
    half, width = bottom.shape[0] - AUX, bottom.shape[1]
    rows = 2 * half + AUX
    return pl.pallas_call(
        functools.partial(finish_kernel, features),
        in_specs=[pl.BlockSpec(memory_space=pltpu.SMEM)] + whole_vmem(7),
        out_specs=pl.BlockSpec(memory_space=pltpu.VMEM),
        scratch_shapes=[pltpu.VMEM((rows, width), BF16), pltpu.VMEM((2, 2 * half, HEAD), F32)],
        out_shape=jax.ShapeDtypeStruct((3, 2 * half, width), BF16),
        compiler_params=params(16),
        cost_estimate=cost(4e9, 4 * MIB),
        name="finish",
    )(source, weight, top, bottom, *state, gains)


def attend_kernel(place, qkv, out):
    tile = 512
    rows, width = out.shape
    for lane in range(0, width, HEAD):
        lanes = slice(lane, lane + HEAD)
        keys, values = qkv[1, :, lanes], qkv[2, :, lanes]
        for first in range(0, rows, tile):
            queries = qkv[0, pl.ds(pl.multiple_of(place[0] * rows + first, tile), tile), lanes]
            scores = lax.dot_general(queries, keys, (((1,), (1,)), ((), ())), preferred_element_type=F32)
            weights = jnp.exp2(scores - jnp.max(scores, axis=1, keepdims=True))
            total = jnp.sum(weights, axis=1, keepdims=True)
            mixed = jnp.dot(weights.astype(BF16), values, preferred_element_type=F32) / total
            out[first : first + tile, lanes] = mixed.astype(BF16)


def attend(qkv, place):
    _, length, width = qkv.shape
    return pl.pallas_call(
        attend_kernel,
        in_specs=[pl.BlockSpec(memory_space=pltpu.SMEM)] + whole_vmem(1),
        out_specs=pl.BlockSpec(memory_space=pltpu.VMEM),
        out_shape=jax.ShapeDtypeStruct((length // 2, width), BF16),
        compiler_params=params(16),
        cost_estimate=cost(4e9, 3 * MIB),
        name="attend",
    )(place, qkv)


def begin_kernel(offset, latents, modulation, top, bottom, gate):
    half, width = top.shape[0] - AUX, top.shape[1]
    top[:half, :] = latents[0, :half, :].astype(BF16)
    bottom[:half, :] = latents[0, half:, :].astype(BF16)
    steps = modulation.shape[1]
    chosen = lax.broadcasted_iota(jnp.int32, (steps, width), 0) == offset[0]
    pick = lambda i: jnp.sum(jnp.where(chosen, modulation[i].astype(F32), 0.0), axis=0, keepdims=True)
    row = lax.broadcasted_iota(jnp.int32, (AUX, width), 0)
    aux = jnp.where(row == 0, pick(1), jnp.where(row == 1, pick(0), 0.0)).astype(BF16)
    top[half:, :] = aux
    bottom[half:, :] = aux
    gate[...] = jnp.broadcast_to(pick(2), gate.shape)


def begin(offset, latents, modulation):
    _, length, width = latents.shape
    piece = jax.ShapeDtypeStruct((length // 2 + AUX, width), BF16)
    return pl.pallas_call(
        begin_kernel,
        in_specs=[SMEM] + whole_vmem(2),
        out_specs=whole_vmem(3),
        out_shape=[piece, piece, jax.ShapeDtypeStruct((8, width), F32)],
        compiler_params=params(16),
        cost_estimate=cost(1e9, 2 * MIB),
        name="begin",
    )(offset, latents, modulation)


def partial_kernel(has_sum, dest, attended, weight, *refs):
    count = len(has_sum)
    width = attended.shape[1]
    sums, outs = refs[:-count], refs[-count:]
    place = 0
    for i in range(count):
        columns = pl.ds(pl.multiple_of(dest[i] * width, width), width)
        total = jnp.dot(attended[...], weight[:, columns], preferred_element_type=F32)
        if has_sum[i]:
            total = total + sums[place][...].astype(F32)
            place += 1
        outs[i][...] = total.astype(BF16)


def partial(attended, weight, dest, sums):
    rows, width = attended.shape
    has_sum = [value is not None for value in sums]
    given = [value for value in sums if value is not None]
    return pl.pallas_call(
        functools.partial(partial_kernel, has_sum),
        in_specs=[pl.BlockSpec(memory_space=pltpu.SMEM)] + whole_vmem(2 + len(given)),
        out_specs=whole_vmem(len(sums)),
        out_shape=[jax.ShapeDtypeStruct((rows, width), BF16)] * len(sums),
        compiler_params=params(16),
        cost_estimate=cost(8e9, 2 * MIB),
        name="partial",
    )(dest, attended, weight, *given)


def update_kernel(places, scalars, own, from_below, from_above, gate, latents, noise, *refs):
    velocity_out, increment_out, x, noise_rows, arrived = refs[-5:]
    rows = own.shape[0]
    held = pl.ds(pl.multiple_of(places[0] * rows, rows), rows)
    copies = [
        pltpu.make_async_copy(latents.at[0, held, :], x, arrived.at[0]),
        pltpu.make_async_copy(noise.at[0, held, :], noise_rows, arrived.at[1]),
    ]
    for copy in copies:
        copy.start()
    branch = own[...].astype(F32) + from_below[...].astype(F32) + from_above[...].astype(F32)
    branch = gate[0:1, :] * branch
    for copy in copies:
        copy.wait()
    velocity = x[...] + branch
    velocity_out[0] = velocity.astype(BF16)
    increment = scalars[1] * x[...] - scalars[0] * velocity + noise_rows[...].astype(F32)
    increment_out[...] = increment.astype(BF16)


def update(place, scalars, own, sums, gate, latents, noise, velocity):
    rows, width = own.shape
    operands = [own, *sums, gate, latents, noise]
    in_specs = [SMEM] + whole_vmem(4) + [HBM, HBM]
    aliases = {}
    if velocity is not None:
        aliases = {2 + len(operands): 0}
        operands.append(velocity)
        in_specs.append(pl.BlockSpec(memory_space=pl.ANY))
    return pl.pallas_call(
        update_kernel,
        grid_spec=pltpu.PrefetchScalarGridSpec(
            num_scalar_prefetch=1,
            grid=(1,),
            in_specs=in_specs,
            out_specs=[pl.BlockSpec((1, rows, width), lambda i, p: (0, p[0], 0))] + whole_vmem(1),
            scratch_shapes=[
                pltpu.VMEM((rows, width), F32),
                pltpu.VMEM((rows, width), BF16),
                pltpu.SemaphoreType.DMA((2,)),
            ],
        ),
        out_shape=[
            jax.ShapeDtypeStruct((1, 2 * rows, width), BF16),
            jax.ShapeDtypeStruct((rows, width), BF16),
        ],
        input_output_aliases=aliases,
        compiler_params=params(16),
        cost_estimate=cost(1e9, 3 * MIB),
        name="update",
    )(place, scalars, *operands)


def vmem_call(kernel, name, out_shape, scalars, *operands):
    return pl.pallas_call(
        kernel,
        in_specs=[pl.BlockSpec(memory_space=pltpu.SMEM)] + whole_vmem(len(operands)),
        out_specs=whole_vmem(len(out_shape)),
        out_shape=out_shape,
        compiler_params=params(8),
        cost_estimate=cost(1e9, MIB),
        name=name,
    )(scalars, *operands)


def chip_sum_kernel(where, kept, other, *pieces):
    rows = pieces[0].shape[0]
    for k in range(SIDE):
        part = pl.ds(pl.multiple_of((where[1] + k) % SIDE * rows, rows), rows)
        pieces[k][...] = (kept[part, :].astype(F32) + other[part, :].astype(F32)).astype(BF16)


def row_sum_kernel(where, *refs):
    total = refs[0][...].astype(F32)
    for ref in refs[1:-1]:
        total = total + ref[...].astype(F32)
    refs[-1][...] = total.astype(BF16)


def prefix_kernel(where, *refs):
    x, y = where[0], where[1]
    sums = [ref[...].astype(F32) for ref in refs[:SIDE]]
    before = jnp.zeros_like(sums[0])
    for k in range(1, SIDE):
        before = before + jnp.where(x >= k, refs[SIDE + k - 1][...].astype(F32), 0.0)
    outs = refs[2 * SIDE - 1 :]
    for k in range(SIDE):
        total = before
        for source in range(SIDE):
            total = total + jnp.where((y + SIDE - source) % SIDE < (y + k) % SIDE, sums[source], 0.0)
        outs[k][...] = total.astype(BF16)


def square_sums(change):
    rows, width = change.shape
    square = jnp.sum((change * change).reshape(rows // 8, 8, width), axis=0)
    total = square[:, :HEAD]
    for lane in range(HEAD, width, HEAD):
        total = total + square[:, lane : lane + HEAD]
    return total


def change_kernel(places, where, *refs):
    mine, (kept, other, x) = refs[:SIDE], refs[SIDE : SIDE + 3]
    updated, sent, squares = refs[SIDE + 3 :]
    rows = mine[0].shape[0]
    y, first_core, first_chip = where[1], where[2] == 0, where[3] == 0
    total = jnp.zeros((8, HEAD), F32)
    for k in range(SIDE):
        part = pl.ds(pl.multiple_of((y + SIDE - k) % SIDE * rows, rows), rows)
        even = mine[k][...].astype(F32)
        odd = even + jnp.where(first_core, kept[part, :], other[part, :]).astype(F32)
        sent[part, :] = jnp.where(first_core, odd, even).astype(BF16)
        own_x = x[0, part, :]
        own = jnp.where(first_core, jnp.where(first_chip, own_x, even), odd)
        updated[0, part, :] = own
        total = total + square_sums(own - own_x)
    squares[...] = total


def change(place, where, mine, kept, other, latents):
    half, width = kept.shape
    block = pl.BlockSpec((1, half, width), lambda i, p: (0, p[0], 0))
    return pl.pallas_call(
        change_kernel,
        grid_spec=pltpu.PrefetchScalarGridSpec(
            num_scalar_prefetch=1,
            grid=(1,),
            in_specs=[SMEM] + whole_vmem(SIDE + 2) + [block],
            out_specs=[block] + whole_vmem(2),
        ),
        out_shape=[
            jax.ShapeDtypeStruct((1, 2 * half, width), F32),
            jax.ShapeDtypeStruct((half, width), BF16),
            jax.ShapeDtypeStruct((8, HEAD), F32),
        ],
        compiler_params=params(16),
        cost_estimate=cost(1e9, 3 * MIB),
        name="change",
    )(place, where, *mine, kept, other, latents)


def put_half_kernel(places, where, received, squares, x, _, updated, totals):
    first = jnp.logical_and(where[2] == 0, where[3] == 0)
    own = jnp.where(first, x[0], received[...].astype(F32))
    updated[0] = own
    total = squares[...] + square_sums(own - x[0])
    for level in range(LEVELS):
        totals[level] = total


def put_half(place, where, received, squares, latents, updated):
    half, width = received.shape
    block = pl.BlockSpec((1, half, width), lambda i, p: (0, p[0], 0))
    return pl.pallas_call(
        put_half_kernel,
        grid_spec=pltpu.PrefetchScalarGridSpec(
            num_scalar_prefetch=1,
            grid=(1,),
            in_specs=[SMEM] + whole_vmem(2) + [block, pl.BlockSpec(memory_space=pl.ANY)],
            out_specs=[block] + whole_vmem(1),
        ),
        out_shape=[
            jax.ShapeDtypeStruct(updated.shape, F32),
            jax.ShapeDtypeStruct((LEVELS, 8, HEAD), F32),
        ],
        input_output_aliases={5: 0},
        compiler_params=params(16),
        cost_estimate=cost(1e9, 2 * MIB),
        name="put_half",
    )(place, where, received, squares, latents, updated)


def exclusive_prefix(kept, other, where):
    half, width = kept.shape
    piece = jax.ShapeDtypeStruct((half // SIDE, width), BF16)
    pieces = vmem_call(chip_sum_kernel, "chip_sum", [piece] * SIDE, where, kept, other)
    sums = [pieces[0]] + [shift_tm(pieces[k], 0, k, 0) for k in range(1, SIDE)]
    row_sum = vmem_call(row_sum_kernel, "row_sum", [piece], where, *sums)[0]
    rows = [shift_tm(row_sum, k, 0, 0) for k in range(1, SIDE)]
    prefixes = vmem_call(prefix_kernel, "prefix", [piece] * SIDE, where, *sums, *rows)
    return [prefixes[0]] + [shift_tm(prefixes[k], 0, k, 0) for k in range(1, SIDE)]


def body(latents, noise, qkv_weight, qk_gains, out_weight, modulation, step_sizes, window_start):
    slot = lax.axis_index("tm")
    level = lax.axis_index("tensor")
    offset = window_start[0] + slot
    step_size = lax.dynamic_index_in_dim(step_sizes, offset, 0, keepdims=False)
    own_rows = latents[0]
    length, width = own_rows.shape
    features = width * LEVELS
    half = length // 2
    at = lambda *offsets: jnp.stack([(level + k) % LEVELS for k in offsets]).astype(jnp.int32)

    top, bottom, gate = begin(offset.reshape(1), latents, jnp.transpose(modulation, (1, 0, 2)))
    core = slot % 2
    where = jnp.stack([slot // (2 * SIDE), slot // 2 % SIDE, core, slot // 2]).astype(jnp.int32)
    given_place, kept_place = (1 - core).reshape(1), core.reshape(1)

    weight = jnp.transpose(qkv_weight, (1, 0, 2))
    up_top, up_bottom, down_top, down_bottom = top, bottom, top, bottom
    state = project([(top, bottom)], at(0), weight, None, 40e9)
    for step in range(1, LEVELS // 2):
        up_top, down_top = shift_z(up_top, 1), shift_z(down_top, -1)
        up_bottom, down_bottom = shift_z(up_bottom, 1), shift_z(down_bottom, -1)
        state = project([(up_top, up_bottom), (down_top, down_bottom)], at(-step, step), weight, state, 40e9)
    last = (shift_z(up_top, 1), shift_z(down_bottom, -1))
    query_scale = math.log2(math.e) / math.sqrt(HEAD)
    gains = jnp.stack([qk_gains[0] * query_scale, qk_gains[1]])
    qkv = finish(last, at(LEVELS // 2), weight, state, gains, features)

    far = LEVELS // 2
    scalars = jnp.stack([step_size, (slot == 0).astype(F32)])
    attended = [attend(qkv, given_place), attend(qkv, kept_place)]
    own, from_below, from_above = [None, None], [None, None], [None, None]
    for step in range(far):
        ahead = far - step
        for part in range(2):
            if step == 0:
                block, own[part] = partial(attended[part], out_weight, at(ahead, 0), [None, None])
                if part == 0:
                    from_below[0] = shift_z(block, 1)
                else:
                    from_above[1] = shift_z(block, -1)
                continue
            blocks = partial(attended[part], out_weight, at(ahead, -ahead), [from_below[part], from_above[part]])
            from_below[part], from_above[part] = shift_z(blocks[0], 1), shift_z(blocks[1], -1)
    velocity, given = update(
        given_place, scalars, own[0], (from_below[0], from_above[0]), gate, latents, noise, None
    )
    other = shift_tm(given, 0, 0, 1)
    velocity, kept = update(
        kept_place, scalars, own[1], (from_below[1], from_above[1]), gate, latents, noise, velocity
    )

    mine = exclusive_prefix(kept, other, where)
    updated, sent, squares = change(kept_place, where, mine, kept, other, latents)
    updated, squares = put_half(given_place, where, shift_tm(sent, 0, 0, 1), squares, latents, updated)
    squares = lax.all_to_all(squares, "tensor", 0, 0, tiled=True)
    slot_err = jnp.sum(squares) / (length * features)
    return updated, velocity, slot_err.reshape(1)


def solution(mesh):
    return jax.shard_map(
        body,
        mesh=mesh,
        in_specs=(
            P("tm", None, "tensor"),
            P("tm", None, "tensor"),
            P(None, None, "tensor"),
            P(None, "tensor"),
            P("tensor", None),
            P(None, None, "tensor"),
            P(),
            P(),
        ),
        out_specs=(P("tm", None, "tensor"), P("tm", None, "tensor"), P("tm")),
        check_vma=False,
    )
```
